32 devices in a mesh: groups: 2 (over x), wide: 8 (over z, y), narrow: 2 (over core).
Axes of the slice: x: 2, y: 2, z: 4, core: 2. Of those that a mesh axis runs over, the one named last changes fastest.
Arguments:
- first_input: bfloat16 [64, 8192], P('groups', 'wide'), parts along dimension 0, may hold values from -6 to 6
- second_input: bfloat16 [64, 8192], P('groups', 'wide'), parts along dimension 0, may hold values from -6 to 6
- norm_gain: bfloat16 [8192], P('wide'), may hold values from 0.099609375 to 1.8984375
- w_query: bfloat16 [8192, 8192], P('wide', 'narrow'), may hold values from -0.05 to 0.05
- w_key: bfloat16 [8192, 512], P('wide', 'narrow'), may hold values from -0.05 to 0.05
- w_value: bfloat16 [8192, 512], P('wide', 'narrow'), may hold values from -0.0625 to 0.0625
- w_output: bfloat16 [8192, 8192], P('narrow', 'wide'), may hold values from -0.0625 to 0.0625
- key_cache: bfloat16 [64, 4, 2048, 128], P(('groups', 'wide'), 'narrow'), parts along dimension 0, may hold values from -400 to 400
- value_cache: bfloat16 [64, 4, 2048, 128], P(('groups', 'wide'), 'narrow'), parts along dimension 0, may hold values from -12 to 12
- lengths: int32 [64], P(('groups', 'wide')), parts along dimension 0, may hold values from 2 to 2048, as said below
- positions: int32 [64], P(('groups', 'wide')), parts along dimension 0, may hold values from 0 to 4095
Outputs:
- first_output: bfloat16 [64, 8192], P('groups', 'wide'), parts along dimension 0
- second_output: bfloat16 [64, 8192], P('groups', 'wide'), parts along dimension 0
The draws below stay inside these ranges and needn't reach their ends.
There are 2 independent parts, one for each index of `groups`. The reference program is written for one: setup_inputs(seed, part) draws one part's arguments, and reference() takes and returns one part's arrays. A program takes and returns all parts, laid end to end along the dimension named above; an argument that names none is the same for every part. Nothing has to cross between parts.
Inputs may be any that keep to these rules, and one draw needn't show every extreme that they name: A request's cache holds lengths of its 2048 slots, from slot 0 on; the other slots are not part of it.
All inputs are finite; a program needn't handle non-finite values.
Results may differ from the reference program's by a relative error of at most 0.012.
Values may be sent and summed in bfloat16 or wider, within the bound.
No kernel may reach another device: no remote copies, remote signals or barrier semaphores. Data moves between devices by JAX's collectives and lax.ppermute only.
A program may use at most 128 MiB of HBM per device.

```python
import math
import jax
import jax.numpy as jnp
from jax import lax

D = 8192
QH = 64
KVH = 4
HD = 128
ROWS_DEV = 4
MAXLEN = 2048
ROWS = 32


WEIGHT_LIMIT = 0.0498046875


def shared_projection(key):
    return jax.random.normal(key, (D, KVH * HD), jnp.float32) * (1.0 / math.sqrt(D))


def draw_w_key(key, part):
    base = shared_projection(key)
    return jnp.clip(base, -WEIGHT_LIMIT, WEIGHT_LIMIT).astype(jnp.bfloat16)


def draw_w_query(key, part):
    base = shared_projection(key)
    key = jax.random.fold_in(key, 9)
    noise = jax.random.normal(key, (D, QH * HD), jnp.float32) * (1.0 / math.sqrt(D))
    grouped = jnp.broadcast_to(base.reshape(D, KVH, 1, HD), (D, KVH, QH // KVH, HD)).reshape(D, QH * HD)
    result = 0.8 * grouped + 0.6 * noise
    return jnp.clip(result, -WEIGHT_LIMIT, WEIGHT_LIMIT).astype(jnp.bfloat16)


def draw_lengths(key, part):
    key = jax.random.fold_in(key, 11)
    key_base, key_factor, key_top = jax.random.split(key, 3)
    base = jax.random.randint(key_base, (ROWS,), 0, MAXLEN - 1)
    factor = jnp.repeat(jax.random.randint(key_factor, (ROWS // ROWS_DEV,), 2, 6), ROWS_DEV)
    result = 2 + base * factor // 5
    chosen = jax.random.randint(key_top, (), 0, ROWS)
    result = jnp.where(jnp.arange(ROWS) == chosen, MAXLEN, result)
    return result.astype(jnp.int32)


def draw_key_cache(key, part):
    key = jax.random.fold_in(key, 7)
    key_base = jax.random.fold_in(key, 0)
    shape = (ROWS, KVH, MAXLEN, HD)
    result = jnp.clip(2.0 * jax.random.normal(key_base, shape, jnp.float32), -12.0, 12.0)
    return result.astype(jnp.bfloat16)


def set_ends(array, rng, smallest, top_value):
    place = [jax.random.randint(jax.random.fold_in(rng, axis), (), 0, length) for axis, length in enumerate(array.shape)]
    longest = array.shape.index(max(array.shape))
    next_to = place[:longest] + [(place[longest] + 1) % array.shape[longest]] + place[longest + 1:]
    return array.at[tuple(place)].set(smallest).at[tuple(next_to)].set(top_value)


def levels(rng, shape, cuts, low, largest):
    def one(position, blocks):
        steps = jax.random.uniform(jax.random.fold_in(jax.random.fold_in(rng, 6), position), (blocks,), jnp.float32, low / len(cuts), largest / len(cuts))
        return jnp.repeat(jnp.exp(steps), shape[position] // blocks).reshape((-1,) + (1,) * (len(shape) - position - 1))

    level = one(*cuts[0])
    for cut in cuts[1:]:
        level = level * one(*cut)
    return level


def normal_values(stream_key, dims, deviation, limit, pieces=(), held_as=jnp.bfloat16):
    values = jax.random.normal(stream_key, dims, jnp.float32) * deviation
    if len(pieces) > 0:
        values = levels(stream_key, dims, pieces, -0.22, 0.18) * values
    return jnp.clip(values, min=-limit, max=limit).astype(held_as)


def setup_inputs(seed: int = 0, part: int = 0) -> dict:
    arg_keys = jax.random.split(jax.random.key(seed), 12)
    own_keys = jax.random.split(jax.random.fold_in(arg_keys[11], part), 12)
    first_input = normal_values(own_keys[0], (ROWS, D), 1.0, 6.0, ((1, 8),))
    second_input = normal_values(own_keys[1], (ROWS, D), 1.0, 6.0, ((1, 8),))
    norm_gain = jnp.clip(1.0 + 0.18 * jax.random.normal(arg_keys[2], (D,), jnp.float32), 0.099609375, 1.8984375).astype(jnp.bfloat16)
    w_query = draw_w_query(jax.random.fold_in(arg_keys[11], 71), part)
    w_key = draw_w_key(jax.random.fold_in(arg_keys[11], 71), part)
    w_value = normal_values(arg_keys[5], (D, KVH * HD), D ** -0.5, 0.0625, ((0, 8), (1, 2)))
    w_output = normal_values(arg_keys[6], (QH * HD, D), (QH * HD) ** -0.5, 0.0625, ((0, 2), (1, 8)))
    key_cache = draw_key_cache(jax.random.fold_in(jax.random.fold_in(arg_keys[11], part), 71), part)
    value_cache = normal_values(own_keys[8], (ROWS, KVH, MAXLEN, HD), 2.0, 12.0, ((0, 8), (1, 2)))
    lengths = draw_lengths(jax.random.fold_in(jax.random.fold_in(arg_keys[11], part), 71), part)
    positions = set_ends(jax.random.randint(own_keys[10], (ROWS,), 0, 2 * MAXLEN), jax.random.fold_in(own_keys[10], 1), 0, (2 * MAXLEN) - 1).astype(jnp.int32)
    return {"first_input": first_input, "second_input": second_input, "norm_gain": norm_gain, "w_query": w_query, "w_key": w_key, "w_value": w_value, "w_output": w_output, "key_cache": key_cache, "value_cache": value_cache, "lengths": lengths, "positions": positions}


EPSILON = 1e-05
THETA = 500000.0
NEGATIVE = -1e+30

def rotate(values, where_at):
    half = values.shape[-1] // 2
    inverse = jnp.exp(jnp.arange(half, dtype=jnp.float32) * (-2.0 * math.log(THETA) / values.shape[-1]))
    angle = where_at.astype(jnp.float32)[:, None, None] * inverse
    cosine = jnp.cos(angle)
    sine = jnp.sin(angle)
    first = values[..., :half]
    second = values[..., half:]
    return jnp.concatenate([first * cosine - second * sine, second * cosine + first * sine], axis=-1)

def project(inputs, norm_gain, w_query, w_key, w_value, where_at):
    wide_in = inputs.astype(jnp.float32)
    sums = lax.optimization_barrier(jnp.sum(wide_in * wide_in, axis=1))
    scale = lax.rsqrt(sums / D + EPSILON)[:, None]
    scaled = (wide_in * norm_gain.astype(jnp.float32)).astype(jnp.bfloat16)
    query = jnp.dot(scaled, w_query, preferred_element_type=jnp.float32) * scale
    keys = jnp.dot(scaled, w_key, preferred_element_type=jnp.float32) * scale
    values = jnp.dot(scaled, w_value, preferred_element_type=jnp.float32) * scale
    query = rotate(query.reshape(ROWS, QH, HD), where_at).astype(jnp.bfloat16)
    keys = rotate(keys.reshape(ROWS, KVH, HD), where_at).astype(jnp.bfloat16)
    values = values.reshape(ROWS, KVH, HD).astype(jnp.bfloat16)
    return (query, keys, values)

def attend_row(operands):
    query, cache_keys, cache_values, length, new_keys, new_values = operands
    grouped = query.reshape(KVH, QH // KVH, HD).astype(jnp.float32)
    scale = 1.0 / math.sqrt(HD)
    cached = jnp.einsum('kgd,ktd->kgt', grouped, cache_keys.astype(jnp.float32)) * scale
    fresh = jnp.einsum('kgd,knd->kgn', grouped, new_keys.astype(jnp.float32)) * scale
    live = (jnp.arange(MAXLEN) < length)[None, None, :]
    cached = jnp.where(live, cached, NEGATIVE)
    top = jnp.maximum(lax.optimization_barrier(jnp.max(cached, axis=-1)), lax.optimization_barrier(jnp.max(fresh, axis=-1)))
    cached_weight = jnp.where(live, jnp.exp(cached - top[..., None]), 0.0)
    fresh_weight = jnp.exp(fresh - top[..., None])
    total = lax.optimization_barrier(jnp.sum(cached_weight, axis=-1)) + lax.optimization_barrier(jnp.sum(fresh_weight, axis=-1))
    mixed = jnp.einsum('kgt,ktd->kgd', cached_weight.astype(jnp.bfloat16).astype(jnp.float32), cache_values.astype(jnp.float32))
    mixed = mixed + jnp.einsum('kgn,knd->kgd', fresh_weight.astype(jnp.bfloat16).astype(jnp.float32), new_values.astype(jnp.float32))
    return (mixed / total[..., None]).astype(jnp.bfloat16).reshape(QH * HD)

def finish(inputs, attended, w_output):
    total = inputs.astype(jnp.float32) + jnp.dot(attended, w_output, preferred_element_type=jnp.float32)
    return total.astype(jnp.bfloat16)

def reference(first_input, second_input, norm_gain, w_query, w_key, w_value, w_output, key_cache, value_cache, lengths, positions):
    query_one, key_one, value_one = project(first_input, norm_gain, w_query, w_key, w_value, positions)
    query_two, key_two, value_two = project(second_input, norm_gain, w_query, w_key, w_value, positions + 1)
    attended_one = lax.map(attend_row, (query_one, key_cache, value_cache, lengths, key_one[:, :, None, :], value_one[:, :, None, :]))
    attended_two = lax.map(attend_row, (query_two, key_cache, value_cache, lengths, jnp.stack([key_one, key_two], axis=2), jnp.stack([value_one, value_two], axis=2)))
    return (finish(first_input, attended_one, w_output), finish(second_input, attended_two, w_output))
```

```python
import functools
import math

import jax
import jax.numpy as jnp
from jax import lax
from jax.experimental import pallas as pl
from jax.experimental.pallas import tpu as pltpu
from jax.sharding import PartitionSpec as P

EPSILON = 1e-05
THETA = 500000.0
NEGATIVE = -1e30
LANES = 128
CHUNK = 512
BLOCK = 512
MIB = 1 << 20

F32 = jnp.float32
BF16 = jnp.bfloat16


def one_hot(shape, order_axis, place, order, outer, rows_dev, rows):
    inner = order.shape[0]
    ranked = lax.broadcasted_iota(jnp.int32, shape, order_axis)
    row = lax.broadcasted_iota(jnp.int32, shape, 1 - order_axis)
    request = lax.rem(ranked, rows_dev)
    token = lax.rem(ranked // rows_dev, 2)
    step = ranked // (2 * rows_dev)
    outer_step = lax.rem(step, outer)
    inner_step = step // outer
    offset = jnp.zeros(shape, jnp.int32)
    for index in range(inner):
        offset = jnp.where(inner_step == index, order[index], offset)
    device = jnp.bitwise_xor(place, offset + inner * outer_step)
    source = token * rows + device * rows_dev + request
    return (row == source).astype(BF16)


def project_kernel(
    rows_dev, outer, place, order, first, second, gain, w_query, w_key, w_value, keep, *rest
):
    sends, (chunks, scaled, sems) = rest[:-3], rest[-3:]
    rows, depth = first.shape
    count = chunks.shape[0]
    heads_width = w_query.shape[1]
    kv_width = w_key.shape[1]

    def fetch(index):
        return pltpu.make_async_copy(
            w_query.at[:, pl.ds(index * CHUNK, CHUNK)], chunks.at[index], sems.at[index]
        )

    for index in range(count):
        fetch(index).start()
    block = keep.shape[0]
    pick = one_hot((2 * rows, 2 * rows), 0, place[0], order, outer, rows_dev, rows)
    stacked = jnp.concatenate([first[...], second[...]], axis=0)
    ordered = jnp.dot(pick, stacked, preferred_element_type=F32)
    squares = jnp.sum(ordered * ordered, axis=1, keepdims=True)
    scaled[...] = (ordered * gain[...].astype(F32)).astype(BF16)

    def put(start, width, value):
        keep[:, start : start + width] = value[:block]
        for index, send in enumerate(sends):
            begin = (index + 1) * block
            send[:, start : start + width] = value[begin : begin + block].astype(BF16)

    end = heads_width + 2 * kv_width
    high = squares.astype(BF16).astype(F32)
    lane = lax.broadcasted_iota(jnp.int32, (2 * rows, LANES), 1)
    coded = jnp.where(lax.rem(lane, 2) == 0, high, squares - high)
    keep[:, end : end + LANES] = jnp.broadcast_to(squares[:block], (block, LANES))
    for index, send in enumerate(sends):
        begin = (index + 1) * block
        send[:, end : end + LANES] = coded[begin : begin + block].astype(BF16)
    put(heads_width, kv_width, jnp.dot(scaled[...], w_key[...], preferred_element_type=F32))
    put(
        heads_width + kv_width,
        kv_width,
        jnp.dot(scaled[...], w_value[...], preferred_element_type=F32),
    )
    for index in range(count):
        fetch(index).wait()
        put(
            index * CHUNK,
            CHUNK,
            jnp.dot(scaled[...], chunks[index], preferred_element_type=F32),
        )


def decoded(tail):
    wide = tail.astype(F32)
    return wide + pltpu.roll(wide, 1, 1)


def combine_kernel(parts, outer, keep, *refs):
    received, (mine, *sends) = refs[:parts], refs[parts:]
    width = keep.shape[1] - LANES
    block = keep.shape[0] // outer
    total = keep[:, :width]
    tail = keep[:, width:]
    for part in received:
        total = total + part[:, :width].astype(F32)
        tail = tail + decoded(part[:, width:])
    mine[:, :width] = total[:block]
    mine[:, width:] = tail[:block]
    high = tail.astype(BF16).astype(F32)
    lane = lax.broadcasted_iota(jnp.int32, tail.shape, 1)
    coded = jnp.where(lax.rem(lane, 2) == 0, high, tail - high)
    for index, send in enumerate(sends):
        begin = (index + 1) * block
        send[:, :width] = total[begin : begin + block].astype(BF16)
        send[:, width:] = coded[begin : begin + block].astype(BF16)


def attend_kernel(parts, model_width, lengths, mine, *refs):
    received = refs[:parts]
    cosine, sine, key_cache, value_cache, attended, queries, new_keys, new_values, results = refs[
        parts:
    ]
    rows_dev, kv_heads, max_length, width = key_cache.shape
    heads = queries.shape[0]
    group = heads // kv_heads
    both = mine.shape[0]
    end = mine.shape[1] - LANES
    tail = mine[:, end:]
    for part in received:
        tail = tail + decoded(part[:, end:])
    scale = lax.rsqrt(tail / model_width + EPSILON)

    def head(index):
        columns = slice(index * width, (index + 1) * width)
        value = mine[:, columns]
        for part in received:
            value = value + part[:, columns].astype(F32)
        return value * scale

    def rotate(value):
        return value * cosine[...] + pltpu.roll(value, width // 2, 1) * sine[...]

    for index in range(heads):
        queries[index] = rotate(head(index))
    blank = jnp.zeros((both, width), F32)
    for index in range(kv_heads):
        new_keys[index] = jnp.concatenate([rotate(head(heads + index)), blank], axis=0).astype(BF16)
        new_values[index] = jnp.concatenate(
            [head(heads + kv_heads + index), blank], axis=0
        ).astype(BF16)

    factor = 1.0 / math.sqrt(width)
    contract = (((1,), (1,)), ((), ()))

    def request(row, blocks):
        length = lengths[row]
        span = blocks * BLOCK
        for index in range(kv_heads):
            pick = pl.ds(index * group, group)
            query = jnp.concatenate(
                [queries[pick, row, :], queries[pick, rows_dev + row, :]], axis=0
            ).astype(BF16)
            fresh = (
                lax.dot_general(query, new_keys[index], contract, preferred_element_type=F32)
                * factor
            )
            slot = lax.broadcasted_iota(jnp.int32, fresh.shape, 1)
            token = lax.broadcasted_iota(jnp.int32, fresh.shape, 0) // group
            seen = (
                (lax.rem(slot, rows_dev) == row) & (slot // rows_dev <= token) & (slot < both)
            )
            fresh = jnp.where(seen, fresh, NEGATIVE)
            scores = (
                lax.dot_general(
                    query, key_cache[row, index, :span, :], contract, preferred_element_type=F32
                )
                * factor
            )
            live = lax.broadcasted_iota(jnp.int32, scores.shape, 1) < length
            scores = jnp.where(live, scores, NEGATIVE)
            top = jnp.maximum(
                jnp.max(scores, axis=1, keepdims=True), jnp.max(fresh, axis=1, keepdims=True)
            )
            weight = jnp.exp(scores - top)
            fresh = jnp.exp(fresh - top)
            total = jnp.sum(weight, axis=1, keepdims=True) + jnp.sum(fresh, axis=1, keepdims=True)
            mixed = jnp.dot(
                weight.astype(BF16), value_cache[row, index, :span, :], preferred_element_type=F32
            ) + jnp.dot(fresh.astype(BF16), new_values[index], preferred_element_type=F32)
            mixed = mixed / total
            results[pick, row, :] = mixed[:group]
            results[pick, rows_dev + row, :] = mixed[group:]

    limit = max_length // BLOCK

    @pl.loop(0, rows_dev)
    def _(row):
        needed = pl.cdiv(lengths[row], BLOCK)
        for blocks in range(1, limit + 1):

            @pl.when(needed == blocks)
            def _():
                request(row, blocks)

    for index in range(heads):
        attended[:, index * width : (index + 1) * width] = results[index].astype(BF16)


def output_kernel(rows_dev, outer, place, order, *refs):
    gathered, (w_output, out) = refs[:-2], refs[-2:]
    count = out.shape[0]
    stacked = jnp.concatenate([part[...] for part in gathered], axis=0)
    back = one_hot((count, count), 1, place[0], order, outer, rows_dev, count // 2)
    attended = jnp.dot(back, stacked, preferred_element_type=F32).astype(BF16)
    out[...] = jnp.dot(attended, w_output[...], preferred_element_type=F32)


def whole(space=pltpu.VMEM):
    return pl.BlockSpec(memory_space=space)


def rotary(positions, width):
    half = width // 2
    inverse = jnp.exp(jnp.arange(half, dtype=F32) * (-2.0 * math.log(THETA) / width))
    where_at = jnp.concatenate([positions, positions + 1]).astype(F32)
    angle = where_at[:, None] * inverse
    cosine = jnp.cos(angle)
    sine = jnp.sin(angle)
    return (
        jnp.concatenate([cosine, cosine], axis=1),
        jnp.concatenate([-sine, sine], axis=1),
    )


def on_device(
    first_input,
    second_input,
    norm_gain,
    w_query,
    w_key,
    w_value,
    w_output,
    key_cache,
    value_cache,
    lengths,
    positions,
):
    devices = lax.axis_size("wide")
    cores = lax.axis_size("narrow")
    rows_dev, kv_heads, _, width = key_cache.shape
    rows, depth = first_input.shape
    inner = math.gcd(devices, 4)
    outer = devices // inner
    both = 2 * rows_dev
    block = outer * both
    heads = w_query.shape[1] // width
    columns = w_query.shape[1] + 2 * w_key.shape[1] + LANES

    plans = ([0, 1, 3, 2], [0, 2, 3, 1]) if inner == 4 else (list(range(inner)),) * 2
    gather_plans = ([0, 3, 1, 2], [0, 3, 2, 1]) if inner == 4 else plans
    core = lax.axis_index("narrow")
    place = lax.axis_index("wide").reshape(1).astype(jnp.int32)

    def order_of(plan):
        return jnp.where(core == 0, jnp.array(plan[0], jnp.int32), jnp.array(plan[1], jnp.int32))

    def exchange(value, steps):
        pairs = [
            (place_from * cores + c, (place_from ^ steps[min(c, 1)]) * cores + c)
            for c in range(cores)
            for place_from in range(devices)
        ]
        return lax.ppermute(value, ("wide", "narrow"), pairs)

    order = order_of(plans)
    chunks = w_query.shape[1] // CHUNK
    keep, *sends = pl.pallas_call(
        functools.partial(project_kernel, rows_dev, outer),
        out_shape=[jax.ShapeDtypeStruct((block, columns), F32)]
        + [jax.ShapeDtypeStruct((block, columns), BF16)] * (inner - 1),
        in_specs=[whole(pltpu.SMEM)] * 2
        + [whole()] * 3
        + [whole(pltpu.HBM)]
        + [whole()] * 2,
        out_specs=[whole()] * inner,
        scratch_shapes=[
            pltpu.VMEM((chunks, depth, CHUNK), BF16),
            pltpu.VMEM((2 * rows, depth), BF16),
            pltpu.SemaphoreType.DMA((chunks,)),
        ],
        compiler_params=pltpu.CompilerParams(vmem_limit_bytes=24 * MIB),
        cost_estimate=pl.CostEstimate(
            flops=4 * rows * depth * columns,
            bytes_accessed=2 * depth * columns,
            transcendentals=0,
        ),
        name="project",
    )(place, order, first_input, second_input, norm_gain[None, :], w_query, w_key, w_value)

    received = [
        exchange(send, (plans[0][index + 1], plans[1][index + 1]))
        for index, send in enumerate(sends)
    ]
    mine, *sends = pl.pallas_call(
        functools.partial(combine_kernel, inner - 1, outer),
        out_shape=[jax.ShapeDtypeStruct((both, columns), F32)]
        + [jax.ShapeDtypeStruct((both, columns), BF16)] * (outer - 1),
        in_specs=[whole()] * inner,
        out_specs=[whole()] * outer,
        compiler_params=pltpu.CompilerParams(vmem_limit_bytes=16 * MIB),
        name="combine",
    )(keep, *received)
    received = [
        exchange(send, (inner * (index + 1),) * 2) for index, send in enumerate(sends)
    ]

    cosine, sine = rotary(positions, width)
    attended = pl.pallas_call(
        functools.partial(attend_kernel, outer - 1, devices * depth),
        out_shape=jax.ShapeDtypeStruct((both, heads * width), BF16),
        in_specs=[whole(pltpu.SMEM)] + [whole()] * (outer + 4),
        out_specs=whole(),
        scratch_shapes=[
            pltpu.VMEM((heads, both, width), F32),
            pltpu.VMEM((kv_heads, 2 * both, width), BF16),
            pltpu.VMEM((kv_heads, 2 * both, width), BF16),
            pltpu.VMEM((heads, both, width), F32),
        ],
        compiler_params=pltpu.CompilerParams(vmem_limit_bytes=32 * MIB),
        name="attend",
    )(lengths, mine, *received, cosine, sine, key_cache, value_cache)

    near = jnp.concatenate(
        [attended] + [exchange(attended, (inner * step,) * 2) for step in range(1, outer)], axis=0
    )
    gathered = [near] + [
        exchange(near, (gather_plans[0][index], gather_plans[1][index]))
        for index in range(1, inner)
    ]
    part = pl.pallas_call(
        functools.partial(output_kernel, rows_dev, outer),
        out_shape=jax.ShapeDtypeStruct((2 * rows, w_output.shape[1]), F32),
        in_specs=[whole(pltpu.SMEM)] * 2 + [whole()] * (inner + 1),
        out_specs=whole(),
        compiler_params=pltpu.CompilerParams(vmem_limit_bytes=24 * MIB),
        name="output",
    )(place, order_of(gather_plans), *gathered, w_output)
    total = part + lax.ppermute(part, "narrow", [(c, c ^ 1) for c in range(cores)])
    return (
        (first_input.astype(F32) + total[:rows]).astype(BF16),
        (second_input.astype(F32) + total[rows:]).astype(BF16),
    )


def solution(mesh):
    return jax.shard_map(
        on_device,
        mesh=mesh,
        in_specs=(
            P("groups", "wide"),
            P("groups", "wide"),
            P("wide"),
            P("wide", "narrow"),
            P("wide", "narrow"),
            P("wide", "narrow"),
            P("narrow", "wide"),
            P(("groups", "wide"), "narrow", None, None),
            P(("groups", "wide"), "narrow", None, None),
            P(("groups", "wide")),
            P(("groups", "wide")),
        ),
        out_specs=(P("groups", "wide"), P("groups", "wide")),
        check_vma=False,
    )
```

```python
import functools
import math

import jax
import jax.numpy as jnp
from jax import lax
from jax.experimental import pallas as pl
from jax.experimental.pallas import tpu as pltpu
from jax.sharding import PartitionSpec as P

EPSILON = 1e-05
THETA = 500000.0
NEGATIVE = -1e30
LANES = 128
CHUNK = 512
BLOCK = 512
MIB = 1 << 20

F32 = jnp.float32
BF16 = jnp.bfloat16


def one_hot(shape, order_axis, plans, outer, rows_dev, rows):
    inner = len(plans[0])
    place = lax.axis_index("wide")
    core = lax.axis_index("narrow")
    ranked = lax.broadcasted_iota(jnp.int32, shape, order_axis)
    row = lax.broadcasted_iota(jnp.int32, shape, 1 - order_axis)
    request = lax.rem(ranked, rows_dev)
    token = lax.rem(ranked // rows_dev, 2)
    step = ranked // (2 * rows_dev)
    outer_step = lax.rem(step, outer)
    inner_step = step // outer
    offset = jnp.zeros(shape, jnp.int32)
    for index in range(inner):
        own = jnp.where(core == 0, plans[0][index], plans[1][index])
        offset = jnp.where(inner_step == index, own, offset)
    device = jnp.bitwise_xor(place, offset + inner * outer_step)
    source = token * rows + device * rows_dev + request
    return (row == source).astype(BF16)


def project_kernel(
    rows_dev, outer, plans, first, second, gain, w_query, w_key, w_value, keep, *rest
):
    sends, (chunks, key_part, value_part, tokens, gains, scaled, sems) = rest[:-7], rest[-7:]
    rows, depth = first.shape
    count = chunks.shape[0]
    heads_width = w_query.shape[1]
    kv_width = w_key.shape[1]

    copies = [
        (first, tokens.at[:rows]),
        (second, tokens.at[rows:]),
        (gain, gains),
        (w_key, key_part),
        (w_value, value_part),
    ] + [
        (w_query.at[:, index * CHUNK : (index + 1) * CHUNK], chunks.at[index])
        for index in range(count)
    ]
    copies = [
        pltpu.make_async_copy(source, target, sems.at[index])
        for index, (source, target) in enumerate(copies)
    ]
    for copy in copies:
        copy.start()
    for copy in copies[:3]:
        copy.wait()
    block = keep.shape[0]
    pick = one_hot((2 * rows, 2 * rows), 0, plans, outer, rows_dev, rows)
    ordered = jnp.dot(pick, tokens[...], preferred_element_type=F32)
    squares = jnp.sum(ordered * ordered, axis=1, keepdims=True)
    scaled[...] = (ordered * gains[...].astype(F32)[None, :]).astype(BF16)

    def put(start, width, value):
        keep[:, start : start + width] = value[:block]
        for index, send in enumerate(sends):
            begin = (index + 1) * block
            send[:, start : start + width] = value[begin : begin + block].astype(BF16)

    end = heads_width + 2 * kv_width
    high = squares.astype(BF16).astype(F32)
    lane = lax.broadcasted_iota(jnp.int32, (2 * rows, LANES), 1)
    coded = jnp.where(lax.rem(lane, 2) == 0, high, squares - high)
    keep[:, end : end + LANES] = jnp.broadcast_to(squares[:block], (block, LANES))
    for index, send in enumerate(sends):
        begin = (index + 1) * block
        send[:, end : end + LANES] = coded[begin : begin + block].astype(BF16)
    for index, part in enumerate((key_part, value_part)):
        copies[3 + index].wait()
        put(
            heads_width + index * kv_width,
            kv_width,
            jnp.dot(scaled[...], part[...], preferred_element_type=F32),
        )
    for index in range(count):
        copies[5 + index].wait()
        put(
            index * CHUNK,
            CHUNK,
            jnp.dot(scaled[...], chunks[index], preferred_element_type=F32),
        )


def decoded(tail):
    wide = tail.astype(F32)
    return wide + pltpu.roll(wide, 1, 1)


def combine_kernel(parts, outer, keep, *refs):
    received, (mine, *sends) = refs[:parts], refs[parts:]
    width = keep.shape[1] - LANES
    block = keep.shape[0] // outer
    total = keep[:, :width]
    tail = keep[:, width:]
    for part in received:
        total = total + part[:, :width].astype(F32)
        tail = tail + decoded(part[:, width:])
    mine[:, :width] = total[:block]
    mine[:, width:] = tail[:block]
    high = tail.astype(BF16).astype(F32)
    lane = lax.broadcasted_iota(jnp.int32, tail.shape, 1)
    coded = jnp.where(lax.rem(lane, 2) == 0, high, tail - high)
    for index, send in enumerate(sends):
        begin = (index + 1) * block
        send[:, :width] = total[begin : begin + block].astype(BF16)
        send[:, width:] = coded[begin : begin + block].astype(BF16)


def attend_kernel(parts, model_width, lengths, mine, *refs):
    received = refs[:parts]
    cosine, sine, key_cache, value_cache, attended, queries, new_keys, new_values, results = refs[
        parts:
    ]
    rows_dev, kv_heads, max_length, width = key_cache.shape
    heads = queries.shape[0]
    group = heads // kv_heads
    both = mine.shape[0]
    end = mine.shape[1] - LANES
    tail = mine[:, end:]
    for part in received:
        tail = tail + decoded(part[:, end:])
    scale = lax.rsqrt(tail / model_width + EPSILON)

    def head(index):
        columns = slice(index * width, (index + 1) * width)
        value = mine[:, columns]
        for part in received:
            value = value + part[:, columns].astype(F32)
        return value * scale

    def rotate(value):
        return value * cosine[...] + pltpu.roll(value, width // 2, 1) * sine[...]

    for index in range(heads):
        queries[index] = rotate(head(index))
    blank = jnp.zeros((both, width), F32)
    for index in range(kv_heads):
        new_keys[index] = jnp.concatenate([rotate(head(heads + index)), blank], axis=0).astype(BF16)
        new_values[index] = jnp.concatenate(
            [head(heads + kv_heads + index), blank], axis=0
        ).astype(BF16)

    factor = 1.0 / math.sqrt(width)
    contract = (((1,), (1,)), ((), ()))

    def request(row, blocks):
        length = lengths[row]
        span = blocks * BLOCK
        for index in range(kv_heads):
            pick = pl.ds(index * group, group)
            query = jnp.concatenate(
                [queries[pick, row, :], queries[pick, rows_dev + row, :]], axis=0
            ).astype(BF16)
            fresh = (
                lax.dot_general(query, new_keys[index], contract, preferred_element_type=F32)
                * factor
            )
            slot = lax.broadcasted_iota(jnp.int32, fresh.shape, 1)
            token = lax.broadcasted_iota(jnp.int32, fresh.shape, 0) // group
            seen = (
                (lax.rem(slot, rows_dev) == row) & (slot // rows_dev <= token) & (slot < both)
            )
            fresh = jnp.where(seen, fresh, NEGATIVE)
            scores = (
                lax.dot_general(
                    query, key_cache[row, index, :span, :], contract, preferred_element_type=F32
                )
                * factor
            )
            live = lax.broadcasted_iota(jnp.int32, scores.shape, 1) < length
            scores = jnp.where(live, scores, NEGATIVE)
            top = jnp.maximum(
                jnp.max(scores, axis=1, keepdims=True), jnp.max(fresh, axis=1, keepdims=True)
            )
            weight = jnp.exp(scores - top)
            fresh = jnp.exp(fresh - top)
            total = jnp.sum(weight, axis=1, keepdims=True) + jnp.sum(fresh, axis=1, keepdims=True)
            mixed = jnp.dot(
                weight.astype(BF16), value_cache[row, index, :span, :], preferred_element_type=F32
            ) + jnp.dot(fresh.astype(BF16), new_values[index], preferred_element_type=F32)
            mixed = mixed / total
            results[pick, row, :] = mixed[:group]
            results[pick, rows_dev + row, :] = mixed[group:]

    limit = max_length // BLOCK

    @pl.loop(0, rows_dev)
    def _(row):
        needed = pl.cdiv(lengths[row], BLOCK)
        for blocks in range(1, limit + 1):

            @pl.when(needed == blocks)
            def _():
                request(row, blocks)

    for index in range(heads):
        attended[:, index * width : (index + 1) * width] = results[index].astype(BF16)


def output_kernel(rows_dev, outer, plans, *refs):
    gathered, (w_output, out) = refs[:-2], refs[-2:]
    count = out.shape[0]
    stacked = jnp.concatenate([part[...] for part in gathered], axis=0)
    back = one_hot((count, count), 1, plans, outer, rows_dev, count // 2)
    attended = jnp.dot(back, stacked, preferred_element_type=F32).astype(BF16)
    out[...] = jnp.dot(attended, w_output[...], preferred_element_type=F32)


def whole(space=pltpu.VMEM):
    return pl.BlockSpec(memory_space=space)


def rotary(positions, width):
    half = width // 2
    inverse = jnp.exp(jnp.arange(half, dtype=F32) * (-2.0 * math.log(THETA) / width))
    where_at = jnp.concatenate([positions, positions + 1]).astype(F32)
    angle = where_at[:, None] * inverse
    cosine = jnp.cos(angle)
    sine = jnp.sin(angle)
    return (
        jnp.concatenate([cosine, cosine], axis=1),
        jnp.concatenate([-sine, sine], axis=1),
    )


def on_device(
    first_input,
    second_input,
    norm_gain,
    w_query,
    w_key,
    w_value,
    w_output,
    key_cache,
    value_cache,
    lengths,
    positions,
):
    devices = lax.axis_size("wide")
    cores = lax.axis_size("narrow")
    rows_dev, kv_heads, _, width = key_cache.shape
    rows, depth = first_input.shape
    inner = math.gcd(devices, 4)
    outer = devices // inner
    both = 2 * rows_dev
    block = outer * both
    heads = w_query.shape[1] // width
    columns = w_query.shape[1] + 2 * w_key.shape[1] + LANES

    plans = ([0, 1, 3, 2], [0, 2, 3, 1]) if inner == 4 else (list(range(inner)),) * 2
    gather_plans = ([0, 3, 1, 2], [0, 3, 2, 1]) if inner == 4 else plans
    def exchange(value, steps):
        pairs = [
            (place_from * cores + c, (place_from ^ steps[min(c, 1)]) * cores + c)
            for c in range(cores)
            for place_from in range(devices)
        ]
        return lax.ppermute(value, ("wide", "narrow"), pairs)

    def placed(space, *values):
        return [pltpu.with_memory_space_constraint(value, space) for value in values]

    chunks = w_query.shape[1] // CHUNK
    keep, *sends = pl.pallas_call(
        functools.partial(project_kernel, rows_dev, outer, plans),
        out_shape=[jax.ShapeDtypeStruct((block, columns), F32)]
        + [jax.ShapeDtypeStruct((block, columns), BF16)] * (inner - 1),
        in_specs=[whole(pltpu.HBM)] * 6,
        out_specs=[whole()] * inner,
        scratch_shapes=[
            pltpu.VMEM((chunks, depth, CHUNK), BF16),
            pltpu.VMEM(w_key.shape, BF16),
            pltpu.VMEM(w_value.shape, BF16),
            pltpu.VMEM((2 * rows, depth), BF16),
            pltpu.VMEM((depth,), BF16),
            pltpu.VMEM((2 * rows, depth), BF16),
            pltpu.SemaphoreType.DMA((chunks + 5,)),
        ],
        compiler_params=pltpu.CompilerParams(vmem_limit_bytes=24 * MIB),
        cost_estimate=pl.CostEstimate(
            flops=4 * rows * depth * columns,
            bytes_accessed=2 * depth * columns,
            transcendentals=0,
        ),
        name="project",
    )(*placed(pltpu.HBM, first_input, second_input, norm_gain, w_query, w_key, w_value))

    received = [
        exchange(send, (plans[0][index + 1], plans[1][index + 1]))
        for index, send in enumerate(sends)
    ]
    mine, *sends = pl.pallas_call(
        functools.partial(combine_kernel, inner - 1, outer),
        out_shape=[jax.ShapeDtypeStruct((both, columns), F32)]
        + [jax.ShapeDtypeStruct((both, columns), BF16)] * (outer - 1),
        in_specs=[whole()] * inner,
        out_specs=[whole()] * outer,
        compiler_params=pltpu.CompilerParams(vmem_limit_bytes=16 * MIB),
        name="combine",
    )(keep, *received)
    received = [
        exchange(send, (inner * (index + 1),) * 2) for index, send in enumerate(sends)
    ]

    cosine, sine = rotary(positions, width)
    attended = pl.pallas_call(
        functools.partial(attend_kernel, outer - 1, devices * depth),
        out_shape=jax.ShapeDtypeStruct((both, heads * width), BF16),
        in_specs=[whole(pltpu.SMEM)] + [whole()] * (outer + 4),
        out_specs=whole(),
        scratch_shapes=[
            pltpu.VMEM((heads, both, width), F32),
            pltpu.VMEM((kv_heads, 2 * both, width), BF16),
            pltpu.VMEM((kv_heads, 2 * both, width), BF16),
            pltpu.VMEM((heads, both, width), F32),
        ],
        compiler_params=pltpu.CompilerParams(vmem_limit_bytes=32 * MIB),
        name="attend",
    )(lengths, mine, *received, cosine, sine, *placed(pltpu.VMEM, key_cache, value_cache))

    near = jnp.concatenate(
        [attended] + [exchange(attended, (inner * step,) * 2) for step in range(1, outer)], axis=0
    )
    gathered = [near] + [
        exchange(near, (gather_plans[0][index], gather_plans[1][index]))
        for index in range(1, inner)
    ]
    part = pl.pallas_call(
        functools.partial(output_kernel, rows_dev, outer, gather_plans),
        out_shape=jax.ShapeDtypeStruct((2 * rows, w_output.shape[1]), F32),
        in_specs=[whole()] * (inner + 1),
        out_specs=whole(),
        compiler_params=pltpu.CompilerParams(vmem_limit_bytes=24 * MIB),
        name="output",
    )(*gathered, *placed(pltpu.VMEM, w_output))
    total = part + lax.ppermute(part, "narrow", [(c, c ^ 1) for c in range(cores)])
    return (
        (first_input.astype(F32) + total[:rows]).astype(BF16),
        (second_input.astype(F32) + total[rows:]).astype(BF16),
    )


def solution(mesh):
    return jax.shard_map(
        on_device,
        mesh=mesh,
        in_specs=(
            P("groups", "wide"),
            P("groups", "wide"),
            P("wide"),
            P("wide", "narrow"),
            P("wide", "narrow"),
            P("wide", "narrow"),
            P("narrow", "wide"),
            P(("groups", "wide"), "narrow", None, None),
            P(("groups", "wide"), "narrow", None, None),
            P(("groups", "wide")),
            P(("groups", "wide")),
        ),
        out_specs=(P("groups", "wide"), P("groups", "wide")),
        check_vma=False,
    )
```

```python
import functools
import math

import jax
import jax.numpy as jnp
from jax import lax
from jax.experimental import pallas as pl
from jax.experimental.pallas import tpu as pltpu
from jax.sharding import PartitionSpec as P

EPSILON = 1e-05
THETA = 500000.0
NEGATIVE = -1e30
LANES = 128
CHUNK = 512
MIB = 1 << 20

F32 = jnp.float32
BF16 = jnp.bfloat16


def one_hot(shape, order_axis, plans, outer, rows_dev, rows):
    inner = len(plans[0])
    place = lax.axis_index("wide")
    core = lax.axis_index("narrow")
    ranked = lax.broadcasted_iota(jnp.int32, shape, order_axis)
    row = lax.broadcasted_iota(jnp.int32, shape, 1 - order_axis)
    request = lax.rem(ranked, rows_dev)
    token = lax.rem(ranked // rows_dev, 2)
    step = ranked // (2 * rows_dev)
    outer_step = lax.rem(step, outer)
    inner_step = step // outer
    offset = jnp.zeros(shape, jnp.int32)
    for index in range(inner):
        own = jnp.where(core == 0, plans[0][index], plans[1][index])
        offset = jnp.where(inner_step == index, own, offset)
    device = jnp.bitwise_xor(place, offset + inner * outer_step)
    source = token * rows + device * rows_dev + request
    return (row == source).astype(BF16)


def project_kernel(
    rows_dev, outer, plans, first, second, gain, w_query, w_key, w_value, *rest
):
    outs, (chunks, key_part, value_part, tokens, gains, scaled, sems) = rest[:-7], rest[-7:]
    nears, fars = outs[: len(plans[0])], outs[len(plans[0]) :]
    rows, depth = first.shape
    count = chunks.shape[0]
    heads_width = w_query.shape[1]
    kv_width = w_key.shape[1]

    copies = [
        (first, tokens.at[:rows]),
        (second, tokens.at[rows:]),
        (gain, gains),
        (w_key, key_part),
        (w_value, value_part),
    ] + [
        (w_query.at[:, index * CHUNK : (index + 1) * CHUNK], chunks.at[index])
        for index in range(count)
    ]
    copies = [
        pltpu.make_async_copy(source, target, sems.at[index])
        for index, (source, target) in enumerate(copies)
    ]
    for copy in copies:
        copy.start()
    for copy in copies[:3]:
        copy.wait()
    both = 2 * rows_dev
    block = outer * both
    pick = one_hot((2 * rows, 2 * rows), 0, plans, outer, rows_dev, rows)
    ordered = jnp.dot(pick, tokens[...], preferred_element_type=F32)
    squares = jnp.sum(ordered * ordered, axis=1, keepdims=True)
    scaled[...] = (ordered * gains[...].astype(F32)[None, :]).astype(BF16)

    def put(start, width, value, coded):
        for index, (near, far) in enumerate(zip(nears, fars)):
            begin = index * block
            part = coded if index > 0 else value
            near[:, start : start + width] = part[begin : begin + both].astype(near.dtype)
            far[:, start : start + width] = part[begin + both : begin + block].astype(far.dtype)

    end = heads_width + 2 * kv_width
    put(end, LANES, jnp.broadcast_to(squares, (2 * rows, LANES)), encoded(squares))
    for index, part in enumerate((key_part, value_part)):
        copies[3 + index].wait()
        put(
            heads_width + index * kv_width,
            kv_width,
            *[jnp.dot(scaled[...], part[...], preferred_element_type=F32)] * 2,
        )
    for index in range(count):
        copies[5 + index].wait()
        put(
            index * CHUNK,
            CHUNK,
            *[jnp.dot(scaled[...], chunks[index], preferred_element_type=F32)] * 2,
        )


def encoded(value):
    high = value.astype(BF16).astype(F32)
    lane = lax.broadcasted_iota(jnp.int32, (value.shape[0], LANES), 1)
    return jnp.where(lax.rem(lane, 2) == 0, high, value - high)


def decoded(tail):
    wide = tail.astype(F32)
    return wide + pltpu.roll(wide, 1, 1)


def combine_kernel(parts, keep, *refs):
    received, sends = refs[:parts], refs[parts:]
    width = keep.shape[1] - LANES
    both = sends[0].shape[0]
    total = keep[:, :width]
    tail = keep[:, width:]
    for part in received:
        total = total + part[:, :width].astype(F32)
        tail = tail + decoded(part[:, width:])
    coded = encoded(tail)
    for index, send in enumerate(sends):
        begin = index * both
        send[:, :width] = total[begin : begin + both].astype(BF16)
        send[:, width:] = coded[begin : begin + both].astype(BF16)


def attend_kernel(parts, model_width, lengths, mine, *refs):
    received = refs[:parts]
    (
        cosine,
        sine,
        key_cache,
        value_cache,
        attended,
        queries,
        new_keys,
        new_values,
        results,
        scores,
    ) = refs[parts:]
    rows_dev, kv_heads, _, width = key_cache.shape
    heads = queries.shape[0]
    group = heads // kv_heads
    both = mine.shape[0]
    end = mine.shape[1] - LANES
    tail = mine[:, end:]
    for part in received:
        tail = tail + decoded(part[:, end:])
    scale = lax.rsqrt(tail / model_width + EPSILON)

    def head(index):
        columns = slice(index * width, (index + 1) * width)
        value = mine[:, columns]
        for part in received:
            value = value + part[:, columns].astype(F32)
        return value * scale

    def rotate(value):
        return value * cosine[...] + pltpu.roll(value, width // 2, 1) * sine[...]

    for index in range(heads):
        queries[index] = rotate(head(index))
    blank = jnp.zeros((both, width), F32)
    for index in range(kv_heads):
        new_keys[index] = jnp.concatenate([rotate(head(heads + index)), blank], axis=0).astype(BF16)
        new_values[index] = jnp.concatenate(
            [head(heads + kv_heads + index), blank], axis=0
        ).astype(BF16)

    factor = 1.0 / math.sqrt(width)
    contract = (((1,), (1,)), ((), ()))

    pairs = [(row, index) for row in range(rows_dev) for index in range(kv_heads)]
    tops = []
    fresh = []
    for number, (row, index) in enumerate(pairs):
        pick = slice(index * group, (index + 1) * group)
        query = jnp.concatenate(
            [queries[pick, row, :], queries[pick, rows_dev + row, :]], axis=0
        ).astype(BF16)
        new = lax.dot_general(query, new_keys[index], contract, preferred_element_type=F32) * factor
        slot = lax.broadcasted_iota(jnp.int32, new.shape, 1)
        token = lax.broadcasted_iota(jnp.int32, new.shape, 0) // group
        seen = (lax.rem(slot, rows_dev) == row) & (slot // rows_dev <= token) & (slot < both)
        new = jnp.where(seen, new, NEGATIVE)
        cached = (
            lax.dot_general(query, key_cache[row, index], contract, preferred_element_type=F32)
            * factor
        )
        live = lax.broadcasted_iota(jnp.int32, cached.shape, 1) < lengths[row]
        cached = jnp.where(live, cached, NEGATIVE)
        scores[number] = cached
        tops.append(
            jnp.maximum(
                jnp.max(cached, axis=1, keepdims=True), jnp.max(new, axis=1, keepdims=True)
            )
        )
        fresh.append(new)
    for number, (row, index) in enumerate(pairs):
        pick = slice(index * group, (index + 1) * group)
        weight = jnp.exp(scores[number] - tops[number])
        new = jnp.exp(fresh[number] - tops[number])
        total = jnp.sum(weight, axis=1, keepdims=True) + jnp.sum(new, axis=1, keepdims=True)
        mixed = jnp.dot(
            weight.astype(BF16), value_cache[row, index], preferred_element_type=F32
        ) + jnp.dot(new.astype(BF16), new_values[index], preferred_element_type=F32)
        mixed = mixed / total
        results[pick, row, :] = mixed[:group]
        results[pick, rows_dev + row, :] = mixed[group:]

    for index in range(heads):
        attended[:, index * width : (index + 1) * width] = results[index].astype(BF16)


def output_kernel(rows_dev, outer, plans, gathered, w_output, out):
    count = out.shape[0]
    back = one_hot((count, count), 1, plans, outer, rows_dev, count // 2)
    attended = jnp.dot(back, gathered[...], preferred_element_type=F32).astype(BF16)
    out[...] = jnp.dot(attended, w_output[...], preferred_element_type=F32)


def whole(space=pltpu.VMEM):
    return pl.BlockSpec(memory_space=space)


def rotary(positions, width):
    half = width // 2
    inverse = jnp.exp(jnp.arange(half, dtype=F32) * (-2.0 * math.log(THETA) / width))
    where_at = jnp.concatenate([positions, positions + 1]).astype(F32)
    angle = where_at[:, None] * inverse
    cosine = jnp.cos(angle)
    sine = jnp.sin(angle)
    return (
        jnp.concatenate([cosine, cosine], axis=1),
        jnp.concatenate([-sine, sine], axis=1),
    )


def on_device(
    first_input,
    second_input,
    norm_gain,
    w_query,
    w_key,
    w_value,
    w_output,
    key_cache,
    value_cache,
    lengths,
    positions,
):
    devices = lax.axis_size("wide")
    cores = lax.axis_size("narrow")
    rows_dev, kv_heads, slots, width = key_cache.shape
    rows, depth = first_input.shape
    inner = math.gcd(devices, 4)
    outer = devices // inner
    both = 2 * rows_dev
    block = outer * both
    heads = w_query.shape[1] // width
    columns = w_query.shape[1] + 2 * w_key.shape[1] + LANES

    plans = ([0, 1, 2, 3], [0, 2, 1, 3]) if inner == 4 else (list(range(inner)),) * 2
    gather_plans = ([0, 1, 3, 2], [0, 2, 3, 1]) if inner == 4 else plans
    def exchange(value, steps):
        pairs = [
            (place_from * cores + c, (place_from ^ steps[min(c, 1)]) * cores + c)
            for c in range(cores)
            for place_from in range(devices)
        ]
        return lax.ppermute(value, ("wide", "narrow"), pairs)

    def placed(space, *values):
        return [pltpu.with_memory_space_constraint(value, space) for value in values]

    chunks = w_query.shape[1] // CHUNK
    types = [F32] + [BF16] * (inner - 1)
    near_far = pl.pallas_call(
        functools.partial(project_kernel, rows_dev, outer, plans),
        out_shape=[jax.ShapeDtypeStruct((both, columns), kind) for kind in types]
        + [jax.ShapeDtypeStruct((block - both, columns), kind) for kind in types],
        in_specs=[whole(pltpu.HBM)] * 6,
        out_specs=[whole()] * (2 * inner),
        scratch_shapes=[
            pltpu.VMEM((chunks, depth, CHUNK), BF16),
            pltpu.VMEM(w_key.shape, BF16),
            pltpu.VMEM(w_value.shape, BF16),
            pltpu.VMEM((2 * rows, depth), BF16),
            pltpu.VMEM((depth,), BF16),
            pltpu.VMEM((2 * rows, depth), BF16),
            pltpu.SemaphoreType.DMA((chunks + 5,)),
        ],
        compiler_params=pltpu.CompilerParams(vmem_limit_bytes=24 * MIB),
        cost_estimate=pl.CostEstimate(
            flops=4 * rows * depth * columns,
            bytes_accessed=2 * depth * columns,
            transcendentals=0,
        ),
        name="project",
    )(*placed(pltpu.HBM, first_input, second_input, norm_gain, w_query, w_key, w_value))

    def spread(values, steps):
        return [
            exchange(value, (steps[0][index + 1], steps[1][index + 1]))
            for index, value in enumerate(values)
        ]

    far = spread(near_far[inner + 1 :], plans)
    near = spread(near_far[1:inner], plans)
    sends = pl.pallas_call(
        functools.partial(combine_kernel, inner - 1),
        out_shape=[jax.ShapeDtypeStruct((both, columns), BF16)] * (outer - 1),
        in_specs=[whole()] * inner,
        out_specs=[whole()] * (outer - 1),
        compiler_params=pltpu.CompilerParams(vmem_limit_bytes=16 * MIB),
        name="combine",
    )(near_far[inner], *far)
    received = near + [
        exchange(send, (inner * (index + 1),) * 2) for index, send in enumerate(sends)
    ]

    cosine, sine = rotary(positions, width)
    attended = pl.pallas_call(
        functools.partial(attend_kernel, len(received), devices * depth),
        out_shape=jax.ShapeDtypeStruct((both, heads * width), BF16),
        in_specs=[whole(pltpu.SMEM)] + [whole()] * (len(received) + 5),
        out_specs=whole(),
        scratch_shapes=[
            pltpu.VMEM((heads, both, width), F32),
            pltpu.VMEM((kv_heads, 2 * both, width), BF16),
            pltpu.VMEM((kv_heads, 2 * both, width), BF16),
            pltpu.VMEM((heads, both, width), F32),
            pltpu.VMEM((rows_dev * kv_heads, 2 * heads // kv_heads, slots), F32),
        ],
        compiler_params=pltpu.CompilerParams(vmem_limit_bytes=32 * MIB),
        name="attend",
    )(lengths, near_far[0], *received, cosine, sine, *placed(pltpu.VMEM, key_cache, value_cache))

    far = [exchange(attended, (inner * step,) * 2) for step in range(1, outer)]
    far = jnp.concatenate(far, axis=0)
    own_blocks = spread([attended] * (inner - 1), gather_plans)
    far_blocks = spread([far] * (inner - 1), gather_plans)
    gathered = jnp.concatenate(
        [attended, far]
        + [block for blocks in zip(own_blocks, far_blocks) for block in blocks],
        axis=0,
    )
    part = pl.pallas_call(
        functools.partial(output_kernel, rows_dev, outer, gather_plans),
        out_shape=jax.ShapeDtypeStruct((2 * rows, w_output.shape[1]), F32),
        in_specs=[whole()] * 2,
        out_specs=whole(),
        compiler_params=pltpu.CompilerParams(vmem_limit_bytes=24 * MIB),
        name="output",
    )(gathered, *placed(pltpu.VMEM, w_output))
    total = part + lax.ppermute(part, "narrow", [(c, c ^ 1) for c in range(cores)])
    return (
        (first_input.astype(F32) + total[:rows]).astype(BF16),
        (second_input.astype(F32) + total[rows:]).astype(BF16),
    )


def solution(mesh):
    return jax.shard_map(
        on_device,
        mesh=mesh,
        in_specs=(
            P("groups", "wide"),
            P("groups", "wide"),
            P("wide"),
            P("wide", "narrow"),
            P("wide", "narrow"),
            P("wide", "narrow"),
            P("narrow", "wide"),
            P(("groups", "wide"), "narrow", None, None),
            P(("groups", "wide"), "narrow", None, None),
            P(("groups", "wide")),
            P(("groups", "wide")),
        ),
        out_specs=(P("groups", "wide"), P("groups", "wide")),
        check_vma=False,
    )
```

```python
import functools
import math

import jax
import jax.numpy as jnp
from jax import lax
from jax.experimental import pallas as pl
from jax.experimental.pallas import tpu as pltpu
from jax.sharding import PartitionSpec as P

EPSILON = 1e-05
THETA = 500000.0
NEGATIVE = -1e30
LANES = 128
CHUNK = 512
MIB = 1 << 20

F32 = jnp.float32
BF16 = jnp.bfloat16


def one_hot(shape, order_axis, plans, outer, rows_dev, rows):
    inner = len(plans[0])
    place = lax.axis_index("wide")
    core = lax.axis_index("narrow")
    ranked = lax.broadcasted_iota(jnp.int32, shape, order_axis)
    row = lax.broadcasted_iota(jnp.int32, shape, 1 - order_axis)
    request = lax.rem(ranked, rows_dev)
    token = lax.rem(ranked // rows_dev, 2)
    step = ranked // (2 * rows_dev)
    outer_step = lax.rem(step, outer)
    inner_step = step // outer
    offset = jnp.zeros(shape, jnp.int32)
    for index in range(inner):
        own = jnp.where(core == 0, plans[0][index], plans[1][index])
        offset = jnp.where(inner_step == index, own, offset)
    device = jnp.bitwise_xor(place, offset + inner * outer_step)
    source = token * rows + device * rows_dev + request
    return (row == source).astype(BF16)


def project_kernel(
    rows_dev, outer, plans, first, second, gain, w_query, w_key, w_value, *rest
):
    outs, (chunks, key_part, value_part, tokens, gains, scaled, sems) = rest[:-7], rest[-7:]
    nears, fars = outs[: len(plans[0])], outs[len(plans[0]) :]
    rows, depth = first.shape
    count = chunks.shape[0]
    heads_width = w_query.shape[1]
    kv_width = w_key.shape[1]

    copies = [
        (first, tokens.at[:rows]),
        (second, tokens.at[rows:]),
        (gain, gains),
        (w_key, key_part),
        (w_value, value_part),
    ] + [
        (w_query.at[:, index * CHUNK : (index + 1) * CHUNK], chunks.at[index])
        for index in range(count)
    ]
    copies = [
        pltpu.make_async_copy(source, target, sems.at[index])
        for index, (source, target) in enumerate(copies)
    ]
    for copy in copies:
        copy.start()
    for copy in copies[:3]:
        copy.wait()
    both = 2 * rows_dev
    block = outer * both
    pick = one_hot((2 * rows, 2 * rows), 0, plans, outer, rows_dev, rows)
    ordered = jnp.dot(pick, tokens[...], preferred_element_type=F32)
    squares = jnp.sum(ordered * ordered, axis=1, keepdims=True)
    scaled[...] = (ordered * gains[...].astype(F32)[None, :]).astype(BF16)

    def put(start, width, value, coded):
        for index, (near, far) in enumerate(zip(nears, fars)):
            begin = index * block
            part = coded if index > 0 else value
            near[:, start : start + width] = part[begin : begin + both].astype(near.dtype)
            far[:, start : start + width] = part[begin + both : begin + block].astype(far.dtype)

    end = heads_width + 2 * kv_width
    put(end, LANES, jnp.broadcast_to(squares, (2 * rows, LANES)), encoded(squares))
    for index, part in enumerate((key_part, value_part)):
        copies[3 + index].wait()
        put(
            heads_width + index * kv_width,
            kv_width,
            *[jnp.dot(scaled[...], part[...], preferred_element_type=F32)] * 2,
        )
    for index in range(count):
        copies[5 + index].wait()
        put(
            index * CHUNK,
            CHUNK,
            *[jnp.dot(scaled[...], chunks[index], preferred_element_type=F32)] * 2,
        )


def encoded(value):
    high = value.astype(BF16).astype(F32)
    lane = lax.broadcasted_iota(jnp.int32, (value.shape[0], LANES), 1)
    return jnp.where(lax.rem(lane, 2) == 0, high, value - high)


def decoded(tail):
    wide = tail.astype(F32)
    return wide + pltpu.roll(wide, 1, 1)


def combine_kernel(parts, keep, *refs):
    received, sends = refs[:parts], refs[parts:]
    width = keep.shape[1] - LANES
    both = sends[0].shape[0]
    total = keep[:, :width]
    tail = keep[:, width:]
    for part in received:
        total = total + part[:, :width].astype(F32)
        tail = tail + decoded(part[:, width:])
    coded = encoded(tail)
    for index, send in enumerate(sends):
        begin = index * both
        send[:, :width] = total[begin : begin + both].astype(BF16)
        send[:, width:] = coded[begin : begin + both].astype(BF16)


def attend_kernel(parts, model_width, lengths, mine, *refs):
    received = refs[:parts]
    (
        cosine,
        sine,
        key_cache,
        value_cache,
        attended,
        queries,
        new_keys,
        new_values,
        results,
        scores,
    ) = refs[parts:]
    rows_dev, kv_heads, _, width = key_cache.shape
    heads = queries.shape[0]
    group = heads // kv_heads
    both = mine.shape[0]
    end = mine.shape[1] - LANES
    tail = mine[:, end:]
    for part in received:
        tail = tail + decoded(part[:, end:])
    scale = lax.rsqrt(tail / model_width + EPSILON)

    def head(index):
        columns = slice(index * width, (index + 1) * width)
        value = mine[:, columns]
        for part in received:
            value = value + part[:, columns].astype(F32)
        return value * scale

    def rotate(value):
        return value * cosine[...] + pltpu.roll(value, width // 2, 1) * sine[...]

    for index in range(heads):
        queries[index] = rotate(head(index))
    blank = jnp.zeros((both, width), F32)
    for index in range(kv_heads):
        new_keys[index] = jnp.concatenate([rotate(head(heads + index)), blank], axis=0).astype(BF16)
        new_values[index] = jnp.concatenate(
            [head(heads + kv_heads + index), blank], axis=0
        ).astype(BF16)

    factor = 1.0 / math.sqrt(width)
    contract = (((1,), (1,)), ((), ()))

    pairs = [(row, index) for row in range(rows_dev) for index in range(kv_heads)]
    tops = []
    fresh = []
    for number, (row, index) in enumerate(pairs):
        pick = slice(index * group, (index + 1) * group)
        query = jnp.concatenate(
            [queries[pick, row, :], queries[pick, rows_dev + row, :]], axis=0
        ).astype(BF16)
        new = lax.dot_general(query, new_keys[index], contract, preferred_element_type=F32) * factor
        slot = lax.broadcasted_iota(jnp.int32, new.shape, 1)
        token = lax.broadcasted_iota(jnp.int32, new.shape, 0) // group
        seen = (lax.rem(slot, rows_dev) == row) & (slot // rows_dev <= token) & (slot < both)
        new = jnp.where(seen, new, NEGATIVE)
        cached = (
            lax.dot_general(query, key_cache[row, index], contract, preferred_element_type=F32)
            * factor
        )
        live = lax.broadcasted_iota(jnp.int32, cached.shape, 1) < lengths[row]
        cached = jnp.where(live, cached, NEGATIVE)
        scores[number] = cached
        tops.append(
            jnp.maximum(
                jnp.max(cached, axis=1, keepdims=True), jnp.max(new, axis=1, keepdims=True)
            )
        )
        fresh.append(new)
    for number, (row, index) in enumerate(pairs):
        pick = slice(index * group, (index + 1) * group)
        weight = jnp.exp(scores[number] - tops[number])
        new = jnp.exp(fresh[number] - tops[number])
        total = jnp.sum(weight, axis=1, keepdims=True) + jnp.sum(new, axis=1, keepdims=True)
        mixed = jnp.dot(
            weight.astype(BF16), value_cache[row, index], preferred_element_type=F32
        ) + jnp.dot(new.astype(BF16), new_values[index], preferred_element_type=F32)
        mixed = mixed / total
        results[pick, row, :] = mixed[:group]
        results[pick, rows_dev + row, :] = mixed[group:]

    for index in range(heads):
        attended[:, index * width : (index + 1) * width] = results[index].astype(BF16)


def output_kernel(rows_dev, outer, plans, gathered, w_output, out):
    count = out.shape[0]
    back = one_hot((count, count), 1, plans, outer, rows_dev, count // 2)
    attended = jnp.dot(back, gathered[...], preferred_element_type=F32).astype(BF16)
    out[...] = jnp.dot(attended, w_output[...], preferred_element_type=F32)


def whole(space=pltpu.VMEM):
    return pl.BlockSpec(memory_space=space)


def rotary(positions, width):
    half = width // 2
    inverse = jnp.exp(jnp.arange(half, dtype=F32) * (-2.0 * math.log(THETA) / width))
    where_at = jnp.concatenate([positions, positions + 1]).astype(F32)
    angle = where_at[:, None] * inverse
    cosine = jnp.cos(angle)
    sine = jnp.sin(angle)
    return (
        jnp.concatenate([cosine, cosine], axis=1),
        jnp.concatenate([-sine, sine], axis=1),
    )


def on_device(
    first_input,
    second_input,
    norm_gain,
    w_query,
    w_key,
    w_value,
    w_output,
    key_cache,
    value_cache,
    lengths,
    positions,
):
    devices = lax.axis_size("wide")
    cores = lax.axis_size("narrow")
    rows_dev, kv_heads, slots, width = key_cache.shape
    rows, depth = first_input.shape
    inner = math.gcd(devices, 4)
    outer = devices // inner
    both = 2 * rows_dev
    block = outer * both
    heads = w_query.shape[1] // width
    columns = w_query.shape[1] + 2 * w_key.shape[1] + LANES

    plans = ([0, 3, 1, 2], [0, 3, 1, 2]) if inner == 4 else (list(range(inner)),) * 2
    gather_plans = ([0, 1, 2, 3], [0, 2, 1, 3]) if inner == 4 else plans
    def exchange(value, steps):
        pairs = [
            (place_from * cores + c, (place_from ^ steps[min(c, 1)]) * cores + c)
            for c in range(cores)
            for place_from in range(devices)
        ]
        return lax.ppermute(value, ("wide", "narrow"), pairs)

    def placed(space, *values):
        return [pltpu.with_memory_space_constraint(value, space) for value in values]

    chunks = w_query.shape[1] // CHUNK
    types = [F32] + [BF16] * (inner - 1)
    near_far = pl.pallas_call(
        functools.partial(project_kernel, rows_dev, outer, plans),
        out_shape=[jax.ShapeDtypeStruct((both, columns), kind) for kind in types]
        + [jax.ShapeDtypeStruct((block - both, columns), kind) for kind in types],
        in_specs=[whole(pltpu.HBM)] * 6,
        out_specs=[whole()] * (2 * inner),
        scratch_shapes=[
            pltpu.VMEM((chunks, depth, CHUNK), BF16),
            pltpu.VMEM(w_key.shape, BF16),
            pltpu.VMEM(w_value.shape, BF16),
            pltpu.VMEM((2 * rows, depth), BF16),
            pltpu.VMEM((depth,), BF16),
            pltpu.VMEM((2 * rows, depth), BF16),
            pltpu.SemaphoreType.DMA((chunks + 5,)),
        ],
        compiler_params=pltpu.CompilerParams(vmem_limit_bytes=24 * MIB),
        cost_estimate=pl.CostEstimate(
            flops=4 * rows * depth * columns,
            bytes_accessed=2 * depth * columns,
            transcendentals=0,
        ),
        name="project",
    )(*placed(pltpu.HBM, first_input, second_input, norm_gain, w_query, w_key, w_value))

    def spread(values, steps):
        return [
            exchange(value, (steps[0][index + 1], steps[1][index + 1]))
            for index, value in enumerate(values)
        ]

    far = spread(near_far[inner + 1 :], plans)
    near = spread(near_far[1:inner], plans)
    sends = pl.pallas_call(
        functools.partial(combine_kernel, inner - 1),
        out_shape=[jax.ShapeDtypeStruct((both, columns), BF16)] * (outer - 1),
        in_specs=[whole()] * inner,
        out_specs=[whole()] * (outer - 1),
        compiler_params=pltpu.CompilerParams(vmem_limit_bytes=16 * MIB),
        name="combine",
    )(near_far[inner], *far)
    received = near + [
        exchange(send, (inner * (index + 1),) * 2) for index, send in enumerate(sends)
    ]

    cosine, sine = rotary(positions, width)
    attended = pl.pallas_call(
        functools.partial(attend_kernel, len(received), devices * depth),
        out_shape=jax.ShapeDtypeStruct((both, heads * width), BF16),
        in_specs=[whole(pltpu.SMEM)] + [whole()] * (len(received) + 5),
        out_specs=whole(),
        scratch_shapes=[
            pltpu.VMEM((heads, both, width), F32),
            pltpu.VMEM((kv_heads, 2 * both, width), BF16),
            pltpu.VMEM((kv_heads, 2 * both, width), BF16),
            pltpu.VMEM((heads, both, width), F32),
            pltpu.VMEM((rows_dev * kv_heads, 2 * heads // kv_heads, slots), F32),
        ],
        compiler_params=pltpu.CompilerParams(vmem_limit_bytes=32 * MIB),
        name="attend",
    )(lengths, near_far[0], *received, cosine, sine, *placed(pltpu.VMEM, key_cache, value_cache))

    far = [exchange(attended, (inner * step,) * 2) for step in range(1, outer)]
    far = jnp.concatenate(far, axis=0)
    own_blocks = spread([attended] * (inner - 2), gather_plans)
    far_blocks = spread([far] * (inner - 2), gather_plans)
    near = jnp.concatenate([attended, far], axis=0)
    last = exchange(near, (gather_plans[0][-1], gather_plans[1][-1]))
    gathered = jnp.concatenate(
        [near] + [block for blocks in zip(own_blocks, far_blocks) for block in blocks] + [last],
        axis=0,
    )
    part = pl.pallas_call(
        functools.partial(output_kernel, rows_dev, outer, gather_plans),
        out_shape=jax.ShapeDtypeStruct((2 * rows, w_output.shape[1]), F32),
        in_specs=[whole()] * 2,
        out_specs=whole(),
        compiler_params=pltpu.CompilerParams(vmem_limit_bytes=24 * MIB),
        name="output",
    )(gathered, *placed(pltpu.VMEM, w_output))
    total = part + lax.ppermute(part, "narrow", [(c, c ^ 1) for c in range(cores)])
    return (
        (first_input.astype(F32) + total[:rows]).astype(BF16),
        (second_input.astype(F32) + total[rows:]).astype(BF16),
    )


def solution(mesh):
    return jax.shard_map(
        on_device,
        mesh=mesh,
        in_specs=(
            P("groups", "wide"),
            P("groups", "wide"),
            P("wide"),
            P("wide", "narrow"),
            P("wide", "narrow"),
            P("wide", "narrow"),
            P("narrow", "wide"),
            P(("groups", "wide"), "narrow", None, None),
            P(("groups", "wide"), "narrow", None, None),
            P(("groups", "wide")),
            P(("groups", "wide")),
        ),
        out_specs=(P("groups", "wide"), P("groups", "wide")),
        check_vma=False,
    )
```

```python
import functools
import math

import jax
import jax.numpy as jnp
from jax import lax
from jax.experimental import pallas as pl
from jax.experimental.pallas import tpu as pltpu
from jax.sharding import PartitionSpec as P

EPSILON = 1e-05
THETA = 500000.0
NEGATIVE = -1e30
LANES = 128
CHUNK = 512
MIB = 1 << 20

F32 = jnp.float32
BF16 = jnp.bfloat16


def one_hot(shape, order_axis, plans, outer, rows_dev, rows):
    inner = len(plans[0])
    place = lax.axis_index("wide")
    core = lax.axis_index("narrow")
    ranked = lax.broadcasted_iota(jnp.int32, shape, order_axis)
    row = lax.broadcasted_iota(jnp.int32, shape, 1 - order_axis)
    request = lax.rem(ranked, rows_dev)
    token = lax.rem(ranked // rows_dev, 2)
    step = ranked // (2 * rows_dev)
    outer_step = lax.rem(step, outer)
    inner_step = step // outer
    offset = jnp.zeros(shape, jnp.int32)
    for index in range(inner):
        own = jnp.where(core == 0, plans[0][index], plans[1][index])
        offset = jnp.where(inner_step == index, own, offset)
    device = jnp.bitwise_xor(place, offset + inner * outer_step)
    source = token * rows + device * rows_dev + request
    return (row == source).astype(BF16)


def project_kernel(
    rows_dev, outer, plans, first, second, gain, w_query, w_key, w_value, *rest
):
    outs, (chunks, key_part, value_part, tokens, gains, scaled, sems) = rest[:-7], rest[-7:]
    nears, fars = outs[: len(plans[0])], outs[len(plans[0]) :]
    rows, depth = first.shape
    count = chunks.shape[0]
    heads_width = w_query.shape[1]
    kv_width = w_key.shape[1]

    copies = [
        (first, tokens.at[:rows]),
        (second, tokens.at[rows:]),
        (gain, gains),
        (w_key, key_part),
        (w_value, value_part),
    ] + [
        (w_query.at[:, index * CHUNK : (index + 1) * CHUNK], chunks.at[index])
        for index in range(count)
    ]
    copies = [
        pltpu.make_async_copy(source, target, sems.at[index])
        for index, (source, target) in enumerate(copies)
    ]
    for copy in copies:
        copy.start()
    for copy in copies[:3]:
        copy.wait()
    both = 2 * rows_dev
    block = outer * both
    pick = one_hot((2 * rows, 2 * rows), 0, plans, outer, rows_dev, rows)
    ordered = jnp.dot(pick, tokens[...], preferred_element_type=F32)
    squares = jnp.sum(ordered * ordered, axis=1, keepdims=True)
    scaled[...] = (ordered * gains[...].astype(F32)[None, :]).astype(BF16)

    def put(start, width, value, coded):
        for index, (near, far) in enumerate(zip(nears, fars)):
            begin = index * block
            part = coded if index > 0 else value
            near[:, start : start + width] = part[begin : begin + both].astype(near.dtype)
            far[:, start : start + width] = part[begin + both : begin + block].astype(far.dtype)

    end = heads_width + 2 * kv_width
    put(end, LANES, jnp.broadcast_to(squares, (2 * rows, LANES)), encoded(squares))
    for index, part in enumerate((key_part, value_part)):
        copies[3 + index].wait()
        put(
            heads_width + index * kv_width,
            kv_width,
            *[jnp.dot(scaled[...], part[...], preferred_element_type=F32)] * 2,
        )
    for index in range(count):
        copies[5 + index].wait()
        put(
            index * CHUNK,
            CHUNK,
            *[jnp.dot(scaled[...], chunks[index], preferred_element_type=F32)] * 2,
        )


def encoded(value):
    high = value.astype(BF16).astype(F32)
    lane = lax.broadcasted_iota(jnp.int32, (value.shape[0], LANES), 1)
    return jnp.where(lax.rem(lane, 2) == 0, high, value - high)


def decoded(tail):
    wide = tail.astype(F32)
    return wide + pltpu.roll(wide, 1, 1)


def combine_kernel(parts, keep, *refs):
    received, sends = refs[:parts], refs[parts:]
    width = keep.shape[1] - LANES
    both = sends[0].shape[0]
    total = keep[:, :width]
    tail = keep[:, width:]
    for part in received:
        total = total + part[:, :width].astype(F32)
        tail = tail + decoded(part[:, width:])
    coded = encoded(tail)
    for index, send in enumerate(sends):
        begin = index * both
        send[:, :width] = total[begin : begin + both].astype(BF16)
        send[:, width:] = coded[begin : begin + both].astype(BF16)


def attend_kernel(parts, model_width, bias, mine, *refs):
    received = refs[:parts]
    (
        cosine,
        sine,
        key_cache,
        value_cache,
        attended,
        queries,
        new_keys,
        new_values,
        results,
        scores,
    ) = refs[parts:]
    rows_dev, kv_heads, _, width = key_cache.shape
    heads = queries.shape[0]
    group = heads // kv_heads
    both = mine.shape[0]
    end = mine.shape[1] - LANES
    tail = mine[:, end:]
    for part in received:
        tail = tail + decoded(part[:, end:])
    scale = lax.rsqrt(tail / model_width + EPSILON)

    def head(index):
        columns = slice(index * width, (index + 1) * width)
        value = mine[:, columns]
        for part in received:
            value = value + part[:, columns].astype(F32)
        return value * scale

    def rotate(value):
        return value * cosine[...] + pltpu.roll(value, width // 2, 1) * sine[...]

    for index in range(heads):
        queries[index] = rotate(head(index))
    blank = jnp.zeros((both, width), F32)
    for index in range(kv_heads):
        new_keys[index] = jnp.concatenate([rotate(head(heads + index)), blank], axis=0).astype(BF16)
        new_values[index] = jnp.concatenate(
            [head(heads + kv_heads + index), blank], axis=0
        ).astype(BF16)

    factor = math.log2(math.e) / math.sqrt(width)
    contract = (((1,), (1,)), ((), ()))

    pairs = [(row, index) for row in range(rows_dev) for index in range(kv_heads)]
    tops = []
    fresh = []
    for number, (row, index) in enumerate(pairs):
        pick = slice(index * group, (index + 1) * group)
        query = jnp.concatenate(
            [queries[pick, row, :], queries[pick, rows_dev + row, :]], axis=0
        ).astype(BF16)
        new = lax.dot_general(query, new_keys[index], contract, preferred_element_type=F32)
        slot = lax.broadcasted_iota(jnp.int32, new.shape, 1)
        token = lax.broadcasted_iota(jnp.int32, new.shape, 0) // group
        seen = (lax.rem(slot, rows_dev) == row) & (slot // rows_dev <= token) & (slot < both)
        new = jnp.where(seen, new, NEGATIVE)
        cached = lax.dot_general(
            query, key_cache[row, index], contract, preferred_element_type=F32
        )
        cached = cached + bias[row : row + 1, :]
        scores[number] = cached
        tops.append(
            jnp.maximum(
                jnp.max(cached, axis=1, keepdims=True), jnp.max(new, axis=1, keepdims=True)
            )
        )
        fresh.append(new)
    for number, (row, index) in enumerate(pairs):
        pick = slice(index * group, (index + 1) * group)
        weight = jnp.exp2((scores[number] - tops[number]) * factor)
        new = jnp.exp2((fresh[number] - tops[number]) * factor)
        total = jnp.sum(weight, axis=1, keepdims=True) + jnp.sum(new, axis=1, keepdims=True)
        mixed = jnp.dot(
            weight.astype(BF16), value_cache[row, index], preferred_element_type=F32
        ) + jnp.dot(new.astype(BF16), new_values[index], preferred_element_type=F32)
        mixed = mixed / total
        results[pick, row, :] = mixed[:group]
        results[pick, rows_dev + row, :] = mixed[group:]

    for index in range(heads):
        attended[:, index * width : (index + 1) * width] = results[index].astype(BF16)


def output_kernel(rows_dev, outer, plans, gathered, w_output, out):
    count = out.shape[0]
    back = one_hot((count, count), 1, plans, outer, rows_dev, count // 2)
    attended = jnp.dot(back, gathered[...], preferred_element_type=F32).astype(BF16)
    out[...] = jnp.dot(attended, w_output[...], preferred_element_type=F32)


def whole(space=pltpu.VMEM):
    return pl.BlockSpec(memory_space=space)


def rotary(positions, width):
    half = width // 2
    inverse = jnp.exp(jnp.arange(half, dtype=F32) * (-2.0 * math.log(THETA) / width))
    where_at = jnp.concatenate([positions, positions + 1]).astype(F32)
    angle = where_at[:, None] * inverse
    cosine = jnp.cos(angle)
    sine = jnp.sin(angle)
    return (
        jnp.concatenate([cosine, cosine], axis=1),
        jnp.concatenate([-sine, sine], axis=1),
    )


def on_device(
    first_input,
    second_input,
    norm_gain,
    w_query,
    w_key,
    w_value,
    w_output,
    key_cache,
    value_cache,
    lengths,
    positions,
):
    devices = lax.axis_size("wide")
    cores = lax.axis_size("narrow")
    rows_dev, kv_heads, slots, width = key_cache.shape
    rows, depth = first_input.shape
    inner = math.gcd(devices, 4)
    outer = devices // inner
    both = 2 * rows_dev
    block = outer * both
    heads = w_query.shape[1] // width
    columns = w_query.shape[1] + 2 * w_key.shape[1] + LANES

    plans = ([0, 3, 1, 2], [0, 3, 1, 2]) if inner == 4 else (list(range(inner)),) * 2
    gather_plans = ([0, 1, 2, 3], [0, 2, 1, 3]) if inner == 4 else plans
    def exchange(value, steps):
        pairs = [
            (place_from * cores + c, (place_from ^ steps[min(c, 1)]) * cores + c)
            for c in range(cores)
            for place_from in range(devices)
        ]
        return lax.ppermute(value, ("wide", "narrow"), pairs)

    def placed(space, *values):
        return [pltpu.with_memory_space_constraint(value, space) for value in values]

    chunks = w_query.shape[1] // CHUNK
    types = [F32] + [BF16] * (inner - 1)
    near_far = pl.pallas_call(
        functools.partial(project_kernel, rows_dev, outer, plans),
        out_shape=[jax.ShapeDtypeStruct((both, columns), kind) for kind in types]
        + [jax.ShapeDtypeStruct((block - both, columns), kind) for kind in types],
        in_specs=[whole(pltpu.HBM)] * 6,
        out_specs=[whole()] * (2 * inner),
        scratch_shapes=[
            pltpu.VMEM((chunks, depth, CHUNK), BF16),
            pltpu.VMEM(w_key.shape, BF16),
            pltpu.VMEM(w_value.shape, BF16),
            pltpu.VMEM((2 * rows, depth), BF16),
            pltpu.VMEM((depth,), BF16),
            pltpu.VMEM((2 * rows, depth), BF16),
            pltpu.SemaphoreType.DMA((chunks + 5,)),
        ],
        compiler_params=pltpu.CompilerParams(vmem_limit_bytes=24 * MIB),
        cost_estimate=pl.CostEstimate(
            flops=4 * rows * depth * columns,
            bytes_accessed=2 * depth * columns,
            transcendentals=0,
        ),
        name="project",
    )(*placed(pltpu.HBM, first_input, second_input, norm_gain, w_query, w_key, w_value))

    def spread(values, steps):
        return [
            exchange(value, (steps[0][index + 1], steps[1][index + 1]))
            for index, value in enumerate(values)
        ]

    far = spread(near_far[inner + 1 :], plans)
    near = spread(near_far[1:inner], plans)
    sends = pl.pallas_call(
        functools.partial(combine_kernel, inner - 1),
        out_shape=[jax.ShapeDtypeStruct((both, columns), BF16)] * (outer - 1),
        in_specs=[whole()] * inner,
        out_specs=[whole()] * (outer - 1),
        compiler_params=pltpu.CompilerParams(vmem_limit_bytes=16 * MIB),
        name="combine",
    )(near_far[inner], *far)
    received = near + [
        exchange(send, (inner * (index + 1),) * 2) for index, send in enumerate(sends)
    ]

    cosine, sine = rotary(positions, width)
    slot = lax.broadcasted_iota(jnp.int32, (rows_dev, slots), 1)
    bias = jnp.where(slot < lengths[:, None], 0.0, NEGATIVE)
    attended = pl.pallas_call(
        functools.partial(attend_kernel, len(received), devices * depth),
        out_shape=jax.ShapeDtypeStruct((both, heads * width), BF16),
        in_specs=[whole()] * (len(received) + 6),
        out_specs=whole(),
        scratch_shapes=[
            pltpu.VMEM((heads, both, width), F32),
            pltpu.VMEM((kv_heads, 2 * both, width), BF16),
            pltpu.VMEM((kv_heads, 2 * both, width), BF16),
            pltpu.VMEM((heads, both, width), F32),
            pltpu.VMEM((rows_dev * kv_heads, 2 * heads // kv_heads, slots), F32),
        ],
        compiler_params=pltpu.CompilerParams(vmem_limit_bytes=32 * MIB),
        name="attend",
    )(bias, near_far[0], *received, cosine, sine, *placed(pltpu.VMEM, key_cache, value_cache))

    far = [exchange(attended, (inner * step,) * 2) for step in range(1, outer)]
    far = jnp.concatenate(far, axis=0)
    own_blocks = spread([attended] * (inner - 2), gather_plans)
    far_blocks = spread([far] * (inner - 2), gather_plans)
    near = jnp.concatenate([attended, far], axis=0)
    last = exchange(near, (gather_plans[0][-1], gather_plans[1][-1]))
    gathered = jnp.concatenate(
        [near] + [block for blocks in zip(own_blocks, far_blocks) for block in blocks] + [last],
        axis=0,
    )
    part = pl.pallas_call(
        functools.partial(output_kernel, rows_dev, outer, gather_plans),
        out_shape=jax.ShapeDtypeStruct((2 * rows, w_output.shape[1]), F32),
        in_specs=[whole()] * 2,
        out_specs=whole(),
        compiler_params=pltpu.CompilerParams(vmem_limit_bytes=24 * MIB),
        name="output",
    )(gathered, *placed(pltpu.VMEM, w_output))
    total = part + lax.ppermute(part, "narrow", [(c, c ^ 1) for c in range(cores)])
    return (
        (first_input.astype(F32) + total[:rows]).astype(BF16),
        (second_input.astype(F32) + total[rows:]).astype(BF16),
    )


def solution(mesh):
    return jax.shard_map(
        on_device,
        mesh=mesh,
        in_specs=(
            P("groups", "wide"),
            P("groups", "wide"),
            P("wide"),
            P("wide", "narrow"),
            P("wide", "narrow"),
            P("wide", "narrow"),
            P("narrow", "wide"),
            P(("groups", "wide"), "narrow", None, None),
            P(("groups", "wide"), "narrow", None, None),
            P(("groups", "wide")),
            P(("groups", "wide")),
        ),
        out_specs=(P("groups", "wide"), P("groups", "wide")),
        check_vma=False,
    )
```

```python
import functools
import math

import jax
import jax.numpy as jnp
from jax import lax
from jax.experimental import pallas as pl
from jax.experimental.pallas import tpu as pltpu
from jax.sharding import PartitionSpec as P

EPSILON = 1e-05
THETA = 500000.0
NEGATIVE = -1e30
LANES = 128
CHUNK = 512
MIB = 1 << 20

F32 = jnp.float32
BF16 = jnp.bfloat16
LINK = jnp.float16
LIFT = 16.0
DROP = 0.125


def one_hot(shape, order_axis, plans, outer, rows_dev, rows):
    inner = len(plans[0])
    place = lax.axis_index("wide")
    core = lax.axis_index("narrow")
    ranked = lax.broadcasted_iota(jnp.int32, shape, order_axis)
    row = lax.broadcasted_iota(jnp.int32, shape, 1 - order_axis)
    request = lax.rem(ranked, rows_dev)
    token = lax.rem(ranked // rows_dev, 2)
    step = ranked // (2 * rows_dev)
    outer_step = lax.rem(step, outer)
    inner_step = step // outer
    offset = jnp.zeros(shape, jnp.int32)
    for index in range(inner):
        own = jnp.where(core == 0, plans[0][index], plans[1][index])
        offset = jnp.where(inner_step == index, own, offset)
    device = jnp.bitwise_xor(place, offset + inner * outer_step)
    source = token * rows + device * rows_dev + request
    return (row == source).astype(BF16)


def project_kernel(
    rows_dev, outer, plans, first, second, gain, w_query, w_key, w_value, *rest
):
    outs, (chunks, key_part, value_part, tokens, gains, scaled, sems) = rest[:-7], rest[-7:]
    nears, fars = outs[: len(plans[0])], outs[len(plans[0]) :]
    rows, depth = first.shape
    count = chunks.shape[0]
    heads_width = w_query.shape[1]
    kv_width = w_key.shape[1]

    copies = [
        (first, tokens.at[:rows]),
        (second, tokens.at[rows:]),
        (gain, gains),
        (w_key, key_part),
        (w_value, value_part),
    ] + [
        (w_query.at[:, index * CHUNK : (index + 1) * CHUNK], chunks.at[index])
        for index in range(count)
    ]
    copies = [
        pltpu.make_async_copy(source, target, sems.at[index])
        for index, (source, target) in enumerate(copies)
    ]
    for copy in copies:
        copy.start()
    for copy in copies[:3]:
        copy.wait()
    both = 2 * rows_dev
    block = outer * both
    pick = one_hot((2 * rows, 2 * rows), 0, plans, outer, rows_dev, rows)
    ordered = jnp.dot(pick, tokens[...], preferred_element_type=F32)
    squares = jnp.sum(ordered * ordered, axis=1, keepdims=True) * DROP
    scaled[...] = (ordered * gains[...].astype(F32)[None, :]).astype(BF16) * LIFT

    def put(start, width, value, coded):
        for index, (near, far) in enumerate(zip(nears, fars)):
            begin = index * block
            part = coded if index > 0 else value
            near[:, start : start + width] = part[begin : begin + both].astype(near.dtype)
            far[:, start : start + width] = part[begin + both : begin + block].astype(far.dtype)

    end = heads_width + 2 * kv_width
    put(end, LANES, jnp.broadcast_to(squares, (2 * rows, LANES)), encoded(squares))
    for index, part in enumerate((key_part, value_part)):
        copies[3 + index].wait()
        put(
            heads_width + index * kv_width,
            kv_width,
            *[jnp.dot(scaled[...], part[...], preferred_element_type=F32)] * 2,
        )
    for index in range(count):
        copies[5 + index].wait()
        put(
            index * CHUNK,
            CHUNK,
            *[jnp.dot(scaled[...], chunks[index], preferred_element_type=F32)] * 2,
        )


def encoded(value):
    high = value.astype(BF16).astype(F32)
    lane = lax.broadcasted_iota(jnp.int32, (value.shape[0], LANES), 1)
    return jnp.where(lax.rem(lane, 2) == 0, high, value - high)


def decoded(tail):
    wide = tail.astype(F32)
    return wide + pltpu.roll(wide, 1, 1)


def combine_kernel(parts, keep, *refs):
    received, sends = refs[:parts], refs[parts:]
    width = keep.shape[1] - LANES
    both = sends[0].shape[0]
    total = keep[:, :width]
    tail = keep[:, width:]
    for part in received:
        total = total + part[:, :width].astype(F32)
        tail = tail + decoded(part[:, width:])
    coded = encoded(tail)
    for index, send in enumerate(sends):
        begin = index * both
        send[:, :width] = total[begin : begin + both]
        send[:, width:] = coded[begin : begin + both]


def attend_kernel(parts, model_width, bias, mine, *refs):
    received = refs[:parts]
    (
        cosine,
        sine,
        key_cache,
        value_cache,
        attended,
        queries,
        new_keys,
        new_values,
        results,
        scores,
    ) = refs[parts:]
    rows_dev, kv_heads, _, width = key_cache.shape
    heads = queries.shape[0]
    group = heads // kv_heads
    both = mine.shape[0]
    end = mine.shape[1] - LANES
    tail = mine[:, end:]
    for part in received:
        tail = tail + decoded(part[:, end:])
    scale = lax.rsqrt(tail / (DROP * model_width) + EPSILON) / LIFT

    def head(index):
        columns = slice(index * width, (index + 1) * width)
        value = mine[:, columns]
        for part in received:
            value = value + part[:, columns].astype(F32)
        return value * scale

    def rotate(value):
        return value * cosine[...] + pltpu.roll(value, width // 2, 1) * sine[...]

    for index in range(heads):
        queries[index] = rotate(head(index))
    blank = jnp.zeros((both, width), F32)
    for index in range(kv_heads):
        new_keys[index] = jnp.concatenate([rotate(head(heads + index)), blank], axis=0).astype(BF16)
        new_values[index] = jnp.concatenate(
            [head(heads + kv_heads + index), blank], axis=0
        ).astype(BF16)

    factor = math.log2(math.e) / math.sqrt(width)
    contract = (((1,), (1,)), ((), ()))

    tops = []
    fresh = []
    for row in range(rows_dev):
        own = []
        for index in range(kv_heads):
            pick = slice(index * group, (index + 1) * group)
            own.append(
                jnp.concatenate(
                    [queries[pick, row, :], queries[pick, rows_dev + row, :]], axis=0
                ).astype(BF16)
            )
        cached = jnp.concatenate(
            [
                lax.dot_general(own[index], key_cache[row, index], contract, preferred_element_type=F32)
                for index in range(kv_heads)
            ],
            axis=0,
        )
        cached = cached + bias[row : row + 1, :]
        scores[row] = cached
        new = jnp.concatenate(
            [
                lax.dot_general(own[index], new_keys[index], contract, preferred_element_type=F32)
                for index in range(kv_heads)
            ],
            axis=0,
        )
        slot = lax.broadcasted_iota(jnp.int32, new.shape, 1)
        token = lax.rem(lax.broadcasted_iota(jnp.int32, new.shape, 0) // group, 2)
        seen = (lax.rem(slot, rows_dev) == row) & (slot // rows_dev <= token) & (slot < both)
        new = jnp.where(seen, new, NEGATIVE)
        tops.append(
            jnp.maximum(
                jnp.max(cached, axis=1, keepdims=True), jnp.max(new, axis=1, keepdims=True)
            )
        )
        fresh.append(new)
    for row in range(rows_dev):
        weight = jnp.exp2((scores[row] - tops[row]) * factor)
        new = jnp.exp2((fresh[row] - tops[row]) * factor)
        total = jnp.sum(weight, axis=1, keepdims=True) + jnp.sum(new, axis=1, keepdims=True)
        weight = weight.astype(BF16)
        new = new.astype(BF16)
        values = jnp.concatenate([value_cache[row, index] for index in range(kv_heads)], axis=1)
        mixed = jnp.dot(weight, values, preferred_element_type=F32)
        for index in range(kv_heads):
            pick = slice(index * group, (index + 1) * group)
            span = slice(2 * index * group, 2 * (index + 1) * group)
            part = mixed[span, index * width : (index + 1) * width]
            part = part + jnp.dot(new[span], new_values[index], preferred_element_type=F32)
            part = part / total[span]
            results[pick, row, :] = part[:group]
            results[pick, rows_dev + row, :] = part[group:]

    for index in range(heads):
        attended[:, index * width : (index + 1) * width] = results[index].astype(BF16)


def output_kernel(rows_dev, outer, plans, gathered, w_output, out):
    count = out.shape[0]
    back = one_hot((count, count), 1, plans, outer, rows_dev, count // 2)
    attended = jnp.dot(back, gathered[...], preferred_element_type=F32).astype(BF16)
    out[...] = jnp.dot(attended, w_output[...], preferred_element_type=F32)


def whole(space=pltpu.VMEM):
    return pl.BlockSpec(memory_space=space)


def rotary(positions, width):
    half = width // 2
    inverse = jnp.exp(jnp.arange(half, dtype=F32) * (-2.0 * math.log(THETA) / width))
    where_at = jnp.concatenate([positions, positions + 1]).astype(F32)
    angle = where_at[:, None] * inverse
    cosine = jnp.cos(angle)
    sine = jnp.sin(angle)
    return (
        jnp.concatenate([cosine, cosine], axis=1),
        jnp.concatenate([-sine, sine], axis=1),
    )


def on_device(
    first_input,
    second_input,
    norm_gain,
    w_query,
    w_key,
    w_value,
    w_output,
    key_cache,
    value_cache,
    lengths,
    positions,
):
    devices = lax.axis_size("wide")
    cores = lax.axis_size("narrow")
    rows_dev, kv_heads, slots, width = key_cache.shape
    rows, depth = first_input.shape
    inner = math.gcd(devices, 4)
    outer = devices // inner
    both = 2 * rows_dev
    block = outer * both
    heads = w_query.shape[1] // width
    columns = w_query.shape[1] + 2 * w_key.shape[1] + LANES

    plans = ([0, 3, 1, 2], [0, 3, 1, 2]) if inner == 4 else (list(range(inner)),) * 2
    gather_plans = ([0, 1, 2, 3], [0, 2, 1, 3]) if inner == 4 else plans
    def exchange(value, steps):
        pairs = [
            (place_from * cores + c, (place_from ^ steps[min(c, 1)]) * cores + c)
            for c in range(cores)
            for place_from in range(devices)
        ]
        return lax.ppermute(value, ("wide", "narrow"), pairs)

    def placed(space, *values):
        return [pltpu.with_memory_space_constraint(value, space) for value in values]

    chunks = w_query.shape[1] // CHUNK
    types = [F32] * inner
    near_far = pl.pallas_call(
        functools.partial(project_kernel, rows_dev, outer, plans),
        out_shape=[jax.ShapeDtypeStruct((both, columns), kind) for kind in types]
        + [jax.ShapeDtypeStruct((block - both, columns), kind) for kind in types],
        in_specs=[whole(pltpu.HBM)] * 6,
        out_specs=[whole()] * (2 * inner),
        scratch_shapes=[
            pltpu.VMEM((chunks, depth, CHUNK), BF16),
            pltpu.VMEM(w_key.shape, BF16),
            pltpu.VMEM(w_value.shape, BF16),
            pltpu.VMEM((2 * rows, depth), BF16),
            pltpu.VMEM((depth,), BF16),
            pltpu.VMEM((2 * rows, depth), BF16),
            pltpu.SemaphoreType.DMA((chunks + 5,)),
        ],
        compiler_params=pltpu.CompilerParams(vmem_limit_bytes=24 * MIB),
        cost_estimate=pl.CostEstimate(
            flops=4 * rows * depth * columns,
            bytes_accessed=2 * depth * columns,
            transcendentals=0,
        ),
        name="project",
    )(*placed(pltpu.HBM, first_input, second_input, norm_gain, w_query, w_key, w_value))

    def spread(values, steps):
        return [
            exchange(value, (steps[0][index + 1], steps[1][index + 1]))
            for index, value in enumerate(values)
        ]

    def narrowed(values):
        return [value.astype(LINK) for value in values]

    far = [value.astype(F32) for value in spread(narrowed(near_far[inner + 1 :]), plans)]
    near = [value.astype(F32) for value in spread(narrowed(near_far[1:inner]), plans)]
    sends = pl.pallas_call(
        functools.partial(combine_kernel, inner - 1),
        out_shape=[jax.ShapeDtypeStruct((both, columns), F32)] * (outer - 1),
        in_specs=[whole()] * inner,
        out_specs=[whole()] * (outer - 1),
        compiler_params=pltpu.CompilerParams(vmem_limit_bytes=16 * MIB),
        name="combine",
    )(near_far[inner], *far)
    received = near + [
        exchange(send, (inner * (index + 1),) * 2).astype(F32)
        for index, send in enumerate(narrowed(sends))
    ]

    cosine, sine = rotary(positions, width)
    slot = lax.broadcasted_iota(jnp.int32, (rows_dev, slots), 1)
    bias = jnp.where(slot < lengths[:, None], 0.0, NEGATIVE)
    attended = pl.pallas_call(
        functools.partial(attend_kernel, len(received), devices * depth),
        out_shape=jax.ShapeDtypeStruct((both, heads * width), BF16),
        in_specs=[whole()] * (len(received) + 6),
        out_specs=whole(),
        scratch_shapes=[
            pltpu.VMEM((heads, both, width), F32),
            pltpu.VMEM((kv_heads, 2 * both, width), BF16),
            pltpu.VMEM((kv_heads, 2 * both, width), BF16),
            pltpu.VMEM((heads, both, width), F32),
            pltpu.VMEM((rows_dev, 2 * heads, slots), F32),
        ],
        compiler_params=pltpu.CompilerParams(vmem_limit_bytes=32 * MIB),
        name="attend",
    )(bias, near_far[0], *received, cosine, sine, *placed(pltpu.VMEM, key_cache, value_cache))

    far = [exchange(attended, (inner * step,) * 2) for step in range(1, outer)]
    far = jnp.concatenate(far, axis=0)
    own_blocks = spread([attended] * (inner - 2), gather_plans)
    far_blocks = spread([far] * (inner - 2), gather_plans)
    near = jnp.concatenate([attended, far], axis=0)
    last = exchange(near, (gather_plans[0][-1], gather_plans[1][-1]))
    gathered = jnp.concatenate(
        [near] + [block for blocks in zip(own_blocks, far_blocks) for block in blocks] + [last],
        axis=0,
    )
    part = pl.pallas_call(
        functools.partial(output_kernel, rows_dev, outer, gather_plans),
        out_shape=jax.ShapeDtypeStruct((2 * rows, w_output.shape[1]), F32),
        in_specs=[whole()] * 2,
        out_specs=whole(),
        compiler_params=pltpu.CompilerParams(vmem_limit_bytes=24 * MIB),
        name="output",
    )(gathered, *placed(pltpu.VMEM, w_output))
    part = (part * DROP).astype(LINK)
    other = lax.ppermute(part, "narrow", [(c, cores - 1 - c) for c in range(cores)])
    total = (part.astype(F32) + other.astype(F32)) / DROP
    return (
        (first_input.astype(F32) + total[:rows]).astype(BF16),
        (second_input.astype(F32) + total[rows:]).astype(BF16),
    )


def solution(mesh):
    return jax.shard_map(
        on_device,
        mesh=mesh,
        in_specs=(
            P("groups", "wide"),
            P("groups", "wide"),
            P("wide"),
            P("wide", "narrow"),
            P("wide", "narrow"),
            P("wide", "narrow"),
            P("narrow", "wide"),
            P(("groups", "wide"), "narrow", None, None),
            P(("groups", "wide"), "narrow", None, None),
            P(("groups", "wide")),
            P(("groups", "wide")),
        ),
        out_specs=(P("groups", "wide"), P("groups", "wide")),
        check_vma=False,
    )
```

```python
import functools
import math

import jax
import jax.numpy as jnp
from jax import lax
from jax.experimental import pallas as pl
from jax.experimental.pallas import tpu as pltpu
from jax.sharding import PartitionSpec as P

EPSILON = 1e-05
THETA = 500000.0
NEGATIVE = -1e30
LANES = 128
CHUNK = 512
MIB = 1 << 20

F32 = jnp.float32
BF16 = jnp.bfloat16
LINK = jnp.float16
LIFT = 16.0
DROP = 0.125


def one_hot(shape, order_axis, plans, outer, rows_dev, rows):
    inner = len(plans[0])
    place = lax.axis_index("wide")
    core = lax.axis_index("narrow")
    ranked = lax.broadcasted_iota(jnp.int32, shape, order_axis)
    row = lax.broadcasted_iota(jnp.int32, shape, 1 - order_axis)
    request = lax.rem(ranked, rows_dev)
    token = lax.rem(ranked // rows_dev, 2)
    step = ranked // (2 * rows_dev)
    outer_step = lax.rem(step, outer)
    inner_step = step // outer
    offset = jnp.zeros(shape, jnp.int32)
    for index in range(inner):
        own = jnp.where(core == 0, plans[0][index], plans[1][index])
        offset = jnp.where(inner_step == index, own, offset)
    device = jnp.bitwise_xor(place, offset + inner * outer_step)
    source = token * rows + device * rows_dev + request
    return (row == source).astype(BF16)


def project_kernel(
    rows_dev, outer, plans, first, second, gain, w_query, w_key, w_value, *rest
):
    outs, (chunks, key_part, value_part, tokens, gains, scaled, sems) = rest[:-7], rest[-7:]
    nears, fars = outs[: len(plans[0])], outs[len(plans[0]) :]
    rows, depth = first.shape
    count = chunks.shape[0]
    heads_width = w_query.shape[1]
    kv_width = w_key.shape[1]

    copies = [
        (first, tokens.at[:rows]),
        (second, tokens.at[rows:]),
        (gain, gains),
        (w_key, key_part),
        (w_value, value_part),
    ] + [
        (w_query.at[:, index * CHUNK : (index + 1) * CHUNK], chunks.at[index])
        for index in range(count)
    ]
    copies = [
        pltpu.make_async_copy(source, target, sems.at[index])
        for index, (source, target) in enumerate(copies)
    ]
    for copy in copies:
        copy.start()
    for copy in copies[:3]:
        copy.wait()
    both = 2 * rows_dev
    block = outer * both
    pick = one_hot((2 * rows, 2 * rows), 0, plans, outer, rows_dev, rows)
    ordered = jnp.dot(pick, tokens[...], preferred_element_type=F32)
    squares = jnp.sum(ordered * ordered, axis=1, keepdims=True) * DROP
    scaled[...] = (ordered * gains[...].astype(F32)[None, :]).astype(BF16) * LIFT

    def put(start, width, value, coded):
        for index, (near, far) in enumerate(zip(nears, fars)):
            begin = index * block
            part = coded if index > 0 else value
            near[:, start : start + width] = part[begin : begin + both].astype(near.dtype)
            far[:, start : start + width] = part[begin + both : begin + block].astype(far.dtype)

    end = heads_width + 2 * kv_width
    put(end, LANES, jnp.broadcast_to(squares, (2 * rows, LANES)), encoded(squares))
    for index, part in enumerate((key_part, value_part)):
        copies[3 + index].wait()
        put(
            heads_width + index * kv_width,
            kv_width,
            *[jnp.dot(scaled[...], part[...], preferred_element_type=F32)] * 2,
        )
    for index in range(count):
        copies[5 + index].wait()
        put(
            index * CHUNK,
            CHUNK,
            *[jnp.dot(scaled[...], chunks[index], preferred_element_type=F32)] * 2,
        )


def encoded(value):
    high = value.astype(BF16).astype(F32)
    lane = lax.broadcasted_iota(jnp.int32, (value.shape[0], LANES), 1)
    return jnp.where(lax.rem(lane, 2) == 0, high, value - high)


def decoded(tail):
    wide = tail.astype(F32)
    return wide + pltpu.roll(wide, 1, 1)


def combine_kernel(parts, keep, *refs):
    received, sends = refs[:parts], refs[parts:]
    width = keep.shape[1] - LANES
    both = sends[0].shape[0]
    total = keep[:, :width]
    tail = keep[:, width:]
    for part in received:
        total = total + part[:, :width].astype(F32)
        tail = tail + decoded(part[:, width:])
    coded = encoded(tail)
    for index, send in enumerate(sends):
        begin = index * both
        send[:, :width] = total[begin : begin + both]
        send[:, width:] = coded[begin : begin + both]


def attend_kernel(parts, model_width, bias, mine, *refs):
    received = refs[:parts]
    (
        cosine,
        sine,
        key_cache,
        value_cache,
        attended,
        queries,
        new_keys,
        new_values,
        results,
        scores,
    ) = refs[parts:]
    rows_dev, kv_heads, _, width = key_cache.shape
    heads = queries.shape[0]
    group = heads // kv_heads
    both = mine.shape[0]
    end = mine.shape[1] - LANES
    tail = mine[:, end:]
    for part in received:
        tail = tail + decoded(part[:, end:])
    scale = lax.rsqrt(tail / (DROP * model_width) + EPSILON) / LIFT

    def head(index):
        columns = slice(index * width, (index + 1) * width)
        value = mine[:, columns]
        for part in received:
            value = value + part[:, columns].astype(F32)
        return value * scale

    def rotate(value):
        return value * cosine[...] + pltpu.roll(value, width // 2, 1) * sine[...]

    for index in range(heads):
        queries[index] = rotate(head(index))
    blank = jnp.zeros((both, width), F32)
    for index in range(kv_heads):
        new_keys[index] = jnp.concatenate([rotate(head(heads + index)), blank], axis=0).astype(BF16)
        new_values[index] = jnp.concatenate(
            [head(heads + kv_heads + index), blank], axis=0
        ).astype(BF16)

    factor = math.log2(math.e) / math.sqrt(width)
    contract = (((1,), (1,)), ((), ()))

    tops = []
    fresh = []
    for row in range(rows_dev):
        own = []
        for index in range(kv_heads):
            pick = slice(index * group, (index + 1) * group)
            own.append(
                jnp.concatenate(
                    [queries[pick, row, :], queries[pick, rows_dev + row, :]], axis=0
                ).astype(BF16)
            )
        cached = jnp.concatenate(
            [
                lax.dot_general(own[index], key_cache[row, index], contract, preferred_element_type=F32)
                for index in range(kv_heads)
            ],
            axis=0,
        )
        cached = cached + bias[row : row + 1, :]
        scores[row] = cached
        new = jnp.concatenate(
            [
                lax.dot_general(own[index], new_keys[index], contract, preferred_element_type=F32)
                for index in range(kv_heads)
            ],
            axis=0,
        )
        slot = lax.broadcasted_iota(jnp.int32, new.shape, 1)
        token = lax.rem(lax.broadcasted_iota(jnp.int32, new.shape, 0) // group, 2)
        seen = (lax.rem(slot, rows_dev) == row) & (slot // rows_dev <= token) & (slot < both)
        new = jnp.where(seen, new, NEGATIVE)
        tops.append(
            jnp.maximum(
                jnp.max(cached, axis=1, keepdims=True), jnp.max(new, axis=1, keepdims=True)
            )
        )
        fresh.append(new)
    for row in range(rows_dev):
        weight = jnp.exp2((scores[row] - tops[row]) * factor)
        new = jnp.exp2((fresh[row] - tops[row]) * factor)
        total = jnp.sum(weight, axis=1, keepdims=True) + jnp.sum(new, axis=1, keepdims=True)
        weight = weight.astype(BF16)
        new = new.astype(BF16)
        values = jnp.concatenate([value_cache[row, index] for index in range(kv_heads)], axis=1)
        mixed = jnp.dot(weight, values, preferred_element_type=F32)
        for index in range(kv_heads):
            pick = slice(index * group, (index + 1) * group)
            span = slice(2 * index * group, 2 * (index + 1) * group)
            part = mixed[span, index * width : (index + 1) * width]
            part = part + jnp.dot(new[span], new_values[index], preferred_element_type=F32)
            part = part / total[span]
            results[pick, row, :] = part[:group]
            results[pick, rows_dev + row, :] = part[group:]

    for index in range(heads):
        attended[:, index * width : (index + 1) * width] = results[index].astype(BF16)


def output_kernel(rows_dev, outer, plans, gathered, w_output, out):
    count = out.shape[0]
    back = one_hot((count, count), 1, plans, outer, rows_dev, count // 2)
    attended = jnp.dot(back, gathered[...], preferred_element_type=F32).astype(BF16)
    out[...] = jnp.dot(attended, w_output[...], preferred_element_type=F32)


def whole(space=pltpu.VMEM):
    return pl.BlockSpec(memory_space=space)


def rotary(positions, width):
    half = width // 2
    inverse = jnp.exp(jnp.arange(half, dtype=F32) * (-2.0 * math.log(THETA) / width))
    where_at = jnp.concatenate([positions, positions + 1]).astype(F32)
    angle = where_at[:, None] * inverse
    cosine = jnp.cos(angle)
    sine = jnp.sin(angle)
    return (
        jnp.concatenate([cosine, cosine], axis=1),
        jnp.concatenate([-sine, sine], axis=1),
    )


def on_device(
    first_input,
    second_input,
    norm_gain,
    w_query,
    w_key,
    w_value,
    w_output,
    key_cache,
    value_cache,
    lengths,
    positions,
):
    devices = lax.axis_size("wide")
    cores = lax.axis_size("narrow")
    rows_dev, kv_heads, slots, width = key_cache.shape
    rows, depth = first_input.shape
    inner = math.gcd(devices, 4)
    outer = devices // inner
    both = 2 * rows_dev
    block = outer * both
    heads = w_query.shape[1] // width
    columns = w_query.shape[1] + 2 * w_key.shape[1] + LANES

    plans = ([0, 3, 1, 2], [0, 3, 1, 2]) if inner == 4 else (list(range(inner)),) * 2
    gather_plans = ([0, 2, 1, 3], [0, 2, 1, 3]) if inner == 4 else plans
    def exchange(value, steps):
        pairs = [
            (place_from * cores + c, (place_from ^ steps[min(c, 1)]) * cores + c)
            for c in range(cores)
            for place_from in range(devices)
        ]
        return lax.ppermute(value, ("wide", "narrow"), pairs)

    def placed(space, *values):
        return [pltpu.with_memory_space_constraint(value, space) for value in values]

    chunks = w_query.shape[1] // CHUNK
    types = [F32] * inner
    near_far = pl.pallas_call(
        functools.partial(project_kernel, rows_dev, outer, plans),
        out_shape=[jax.ShapeDtypeStruct((both, columns), kind) for kind in types]
        + [jax.ShapeDtypeStruct((block - both, columns), kind) for kind in types],
        in_specs=[whole(pltpu.HBM)] * 6,
        out_specs=[whole()] * (2 * inner),
        scratch_shapes=[
            pltpu.VMEM((chunks, depth, CHUNK), BF16),
            pltpu.VMEM(w_key.shape, BF16),
            pltpu.VMEM(w_value.shape, BF16),
            pltpu.VMEM((2 * rows, depth), BF16),
            pltpu.VMEM((depth,), BF16),
            pltpu.VMEM((2 * rows, depth), BF16),
            pltpu.SemaphoreType.DMA((chunks + 5,)),
        ],
        compiler_params=pltpu.CompilerParams(vmem_limit_bytes=24 * MIB),
        cost_estimate=pl.CostEstimate(
            flops=4 * rows * depth * columns,
            bytes_accessed=2 * depth * columns,
            transcendentals=0,
        ),
        name="project",
    )(*placed(pltpu.HBM, first_input, second_input, norm_gain, w_query, w_key, w_value))

    def spread(values, steps):
        return [
            exchange(value, (steps[0][index + 1], steps[1][index + 1]))
            for index, value in enumerate(values)
        ]

    def narrowed(values):
        return [value.astype(LINK) for value in values]

    far = [value.astype(F32) for value in spread(narrowed(near_far[inner + 1 :]), plans)]
    near = [value.astype(F32) for value in spread(narrowed(near_far[1:inner]), plans)]
    sends = pl.pallas_call(
        functools.partial(combine_kernel, inner - 1),
        out_shape=[jax.ShapeDtypeStruct((both, columns), F32)] * (outer - 1),
        in_specs=[whole()] * inner,
        out_specs=[whole()] * (outer - 1),
        compiler_params=pltpu.CompilerParams(vmem_limit_bytes=16 * MIB),
        name="combine",
    )(near_far[inner], *far)
    received = near + [
        exchange(send, (inner * (index + 1),) * 2).astype(F32)
        for index, send in enumerate(narrowed(sends))
    ]

    cosine, sine = rotary(positions, width)
    slot = lax.broadcasted_iota(jnp.int32, (rows_dev, slots), 1)
    bias = jnp.where(slot < lengths[:, None], 0.0, NEGATIVE)
    attended = pl.pallas_call(
        functools.partial(attend_kernel, len(received), devices * depth),
        out_shape=jax.ShapeDtypeStruct((both, heads * width), BF16),
        in_specs=[whole()] * (len(received) + 6),
        out_specs=whole(),
        scratch_shapes=[
            pltpu.VMEM((heads, both, width), F32),
            pltpu.VMEM((kv_heads, 2 * both, width), BF16),
            pltpu.VMEM((kv_heads, 2 * both, width), BF16),
            pltpu.VMEM((heads, both, width), F32),
            pltpu.VMEM((rows_dev, 2 * heads, slots), F32),
        ],
        compiler_params=pltpu.CompilerParams(vmem_limit_bytes=32 * MIB),
        name="attend",
    )(bias, near_far[0], *received, cosine, sine, *placed(pltpu.VMEM, key_cache, value_cache))

    far = [exchange(attended, (inner * step,) * 2) for step in range(1, outer)]
    far = jnp.concatenate(far, axis=0)
    own_blocks = spread([attended] * (inner - 2), gather_plans)
    far_blocks = spread([far] * (inner - 2), gather_plans)
    near = jnp.concatenate([attended, far], axis=0)
    last = exchange(near, (gather_plans[0][-1], gather_plans[1][-1]))
    gathered = jnp.concatenate(
        [near] + [block for blocks in zip(own_blocks, far_blocks) for block in blocks] + [last],
        axis=0,
    )
    part = pl.pallas_call(
        functools.partial(output_kernel, rows_dev, outer, gather_plans),
        out_shape=jax.ShapeDtypeStruct((2 * rows, w_output.shape[1]), F32),
        in_specs=[whole()] * 2,
        out_specs=whole(),
        compiler_params=pltpu.CompilerParams(vmem_limit_bytes=24 * MIB),
        name="output",
    )(gathered, *placed(pltpu.VMEM, w_output))
    part = (part * DROP).astype(LINK)
    other = lax.ppermute(part, "narrow", [(c, cores - 1 - c) for c in range(cores)])
    total = (part.astype(F32) + other.astype(F32)) / DROP
    return (
        (first_input.astype(F32) + total[:rows]).astype(BF16),
        (second_input.astype(F32) + total[rows:]).astype(BF16),
    )


def solution(mesh):
    return jax.shard_map(
        on_device,
        mesh=mesh,
        in_specs=(
            P("groups", "wide"),
            P("groups", "wide"),
            P("wide"),
            P("wide", "narrow"),
            P("wide", "narrow"),
            P("wide", "narrow"),
            P("narrow", "wide"),
            P(("groups", "wide"), "narrow", None, None),
            P(("groups", "wide"), "narrow", None, None),
            P(("groups", "wide")),
            P(("groups", "wide")),
        ),
        out_specs=(P("groups", "wide"), P("groups", "wide")),
        check_vma=False,
    )
```

```python
import functools
import math

import jax
import jax.numpy as jnp
from jax import lax
from jax.experimental import pallas as pl
from jax.experimental.pallas import tpu as pltpu
from jax.sharding import PartitionSpec as P

EPSILON = 1e-05
THETA = 500000.0
NEGATIVE = -1e30
LANES = 128
CHUNK = 512
MIB = 1 << 20

F32 = jnp.float32
BF16 = jnp.bfloat16
LINK = jnp.float16
LIFT = 16.0
DROP = 0.125


def one_hot(shape, order_axis, plans, outer, rows_dev, rows):
    inner = len(plans[0])
    place = lax.axis_index("wide")
    core = lax.axis_index("narrow")
    ranked = lax.broadcasted_iota(jnp.int32, shape, order_axis)
    row = lax.broadcasted_iota(jnp.int32, shape, 1 - order_axis)
    request = lax.rem(ranked, rows_dev)
    token = lax.rem(ranked // rows_dev, 2)
    step = ranked // (2 * rows_dev)
    outer_step = lax.rem(step, outer)
    inner_step = step // outer
    offset = jnp.zeros(shape, jnp.int32)
    for index in range(inner):
        own = jnp.where(core == 0, plans[0][index], plans[1][index])
        offset = jnp.where(inner_step == index, own, offset)
    device = jnp.bitwise_xor(place, offset + inner * outer_step)
    source = token * rows + device * rows_dev + request
    return (row == source).astype(BF16)


def project_kernel(
    rows_dev, outer, plans, first, second, gain, w_query, w_key, w_value, *rest
):
    outs, (chunks, key_part, value_part, tokens, gains, scaled, sems) = rest[:-7], rest[-7:]
    nears, fars = outs[: len(plans[0])], outs[len(plans[0]) :]
    rows, depth = first.shape
    count = chunks.shape[0]
    heads_width = w_query.shape[1]
    kv_width = w_key.shape[1]

    copies = [
        (first, tokens.at[:rows]),
        (second, tokens.at[rows:]),
        (gain, gains),
        (w_key, key_part),
        (w_value, value_part),
    ] + [
        (w_query.at[:, index * CHUNK : (index + 1) * CHUNK], chunks.at[index])
        for index in range(count)
    ]
    copies = [
        pltpu.make_async_copy(source, target, sems.at[index])
        for index, (source, target) in enumerate(copies)
    ]
    for copy in copies:
        copy.start()
    for copy in copies[:3]:
        copy.wait()
    both = 2 * rows_dev
    block = outer * both
    pick = one_hot((2 * rows, 2 * rows), 0, plans, outer, rows_dev, rows)
    ordered = jnp.dot(pick, tokens[...], preferred_element_type=F32)
    squares = jnp.sum(ordered * ordered, axis=1, keepdims=True) * DROP
    scaled[...] = (ordered * gains[...].astype(F32)[None, :]).astype(BF16) * LIFT

    def put(start, width, value, coded):
        for index, (near, far) in enumerate(zip(nears, fars)):
            begin = index * block
            part = coded if index > 0 else value
            near[:, start : start + width] = part[begin : begin + both].astype(near.dtype)
            far[:, start : start + width] = part[begin + both : begin + block].astype(far.dtype)

    end = heads_width + 2 * kv_width
    put(end, LANES, jnp.broadcast_to(squares, (2 * rows, LANES)), encoded(squares))
    for index, part in enumerate((key_part, value_part)):
        copies[3 + index].wait()
        put(
            heads_width + index * kv_width,
            kv_width,
            *[jnp.dot(scaled[...], part[...], preferred_element_type=F32)] * 2,
        )
    for index in range(count):
        copies[5 + index].wait()
        put(
            index * CHUNK,
            CHUNK,
            *[jnp.dot(scaled[...], chunks[index], preferred_element_type=F32)] * 2,
        )


def encoded(value):
    high = value.astype(BF16).astype(F32)
    lane = lax.broadcasted_iota(jnp.int32, (value.shape[0], LANES), 1)
    return jnp.where(lax.rem(lane, 2) == 0, high, value - high)


def decoded(tail):
    wide = tail.astype(F32)
    return wide + pltpu.roll(wide, 1, 1)


def combine_kernel(parts, keep, *refs):
    received, sends = refs[:parts], refs[parts:]
    width = keep.shape[1] - LANES
    both = sends[0].shape[0]
    total = keep[:, :width]
    tail = keep[:, width:]
    for part in received:
        total = total + part[:, :width].astype(F32)
        tail = tail + decoded(part[:, width:])
    coded = encoded(tail)
    for index, send in enumerate(sends):
        begin = index * both
        send[:, :width] = total[begin : begin + both]
        send[:, width:] = coded[begin : begin + both]


def attend_kernel(parts, model_width, bias, mine, *refs):
    received = refs[:parts]
    (
        cosine,
        sine,
        key_cache,
        value_cache,
        attended,
        queries,
        new_keys,
        new_values,
        results,
        scores,
        weights,
    ) = refs[parts:]
    rows_dev, kv_heads, _, width = key_cache.shape
    heads = queries.shape[0]
    group = heads // kv_heads
    both = mine.shape[0]
    end = mine.shape[1] - LANES
    tail = mine[:, end:]
    for part in received:
        tail = tail + decoded(part[:, end:])
    scale = lax.rsqrt(tail / (DROP * model_width) + EPSILON) / LIFT

    def head(index):
        columns = slice(index * width, (index + 1) * width)
        value = mine[:, columns]
        for part in received:
            value = value + part[:, columns].astype(F32)
        return value * scale

    def rotate(value):
        return value * cosine[...] + pltpu.roll(value, width // 2, 1) * sine[...]

    for index in range(heads):
        queries[index] = rotate(head(index))
    blank = jnp.zeros((both, width), F32)
    for index in range(kv_heads):
        new_keys[index] = jnp.concatenate([rotate(head(heads + index)), blank], axis=0).astype(BF16)
        new_values[index] = jnp.concatenate(
            [head(heads + kv_heads + index), blank], axis=0
        ).astype(BF16)

    factor = math.log2(math.e) / math.sqrt(width)
    contract = (((1,), (1,)), ((), ()))

    asked = []
    for row in range(rows_dev):
        own = []
        for index in range(kv_heads):
            pick = slice(index * group, (index + 1) * group)
            own.append(
                jnp.concatenate(
                    [queries[pick, row, :], queries[pick, rows_dev + row, :]], axis=0
                ).astype(BF16)
            )
        asked.append(own)
    fresh = []
    for row in range(rows_dev):
        new = jnp.concatenate(
            [
                lax.dot_general(
                    asked[row][index], new_keys[index], contract, preferred_element_type=F32
                )
                for index in range(kv_heads)
            ],
            axis=0,
        )
        slot = lax.broadcasted_iota(jnp.int32, new.shape, 1)
        token = lax.rem(lax.broadcasted_iota(jnp.int32, new.shape, 0) // group, 2)
        seen = (lax.rem(slot, rows_dev) == row) & (slot // rows_dev <= token) & (slot < both)
        fresh.append(jnp.where(seen, new, NEGATIVE))
    tops = []
    for row in range(rows_dev):
        cached = jnp.concatenate(
            [
                lax.dot_general(
                    asked[row][index], key_cache[row, index], contract, preferred_element_type=F32
                )
                for index in range(kv_heads)
            ],
            axis=0,
        )
        cached = cached + bias[row : row + 1, :]
        scores[row] = cached
        tops.append(jnp.max(cached, axis=1, keepdims=True))
    for row in range(rows_dev):
        tops[row] = jnp.maximum(tops[row], jnp.max(fresh[row], axis=1, keepdims=True))
    totals = []
    news = []
    for row in range(rows_dev):
        weight = jnp.exp2((scores[row] - tops[row]) * factor)
        new = jnp.exp2((fresh[row] - tops[row]) * factor)
        totals.append(
            jnp.sum(weight, axis=1, keepdims=True) + jnp.sum(new, axis=1, keepdims=True)
        )
        weights[row] = weight.astype(BF16)
        news.append(new.astype(BF16))
    for row in range(rows_dev):
        new = news[row]
        total = totals[row]
        weight = weights[row]
        values = jnp.concatenate([value_cache[row, index] for index in range(kv_heads)], axis=1)
        mixed = jnp.dot(weight, values, preferred_element_type=F32)
        for index in range(kv_heads):
            pick = slice(index * group, (index + 1) * group)
            span = slice(2 * index * group, 2 * (index + 1) * group)
            part = mixed[span, index * width : (index + 1) * width]
            part = part + jnp.dot(new[span], new_values[index], preferred_element_type=F32)
            part = part / total[span]
            results[pick, row, :] = part[:group]
            results[pick, rows_dev + row, :] = part[group:]

    for index in range(heads):
        attended[:, index * width : (index + 1) * width] = results[index].astype(BF16)


def output_kernel(rows_dev, outer, plans, gathered, w_output, out):
    count = out.shape[0]
    back = one_hot((count, count), 1, plans, outer, rows_dev, count // 2)
    attended = jnp.dot(back, gathered[...], preferred_element_type=F32).astype(BF16)
    out[...] = jnp.dot(attended, w_output[...], preferred_element_type=F32)


def whole(space=pltpu.VMEM):
    return pl.BlockSpec(memory_space=space)


def rotary(positions, width):
    half = width // 2
    inverse = jnp.exp(jnp.arange(half, dtype=F32) * (-2.0 * math.log(THETA) / width))
    where_at = jnp.concatenate([positions, positions + 1]).astype(F32)
    angle = where_at[:, None] * inverse
    cosine = jnp.cos(angle)
    sine = jnp.sin(angle)
    return (
        jnp.concatenate([cosine, cosine], axis=1),
        jnp.concatenate([-sine, sine], axis=1),
    )


def on_device(
    first_input,
    second_input,
    norm_gain,
    w_query,
    w_key,
    w_value,
    w_output,
    key_cache,
    value_cache,
    lengths,
    positions,
):
    devices = lax.axis_size("wide")
    cores = lax.axis_size("narrow")
    rows_dev, kv_heads, slots, width = key_cache.shape
    rows, depth = first_input.shape
    inner = math.gcd(devices, 4)
    outer = devices // inner
    both = 2 * rows_dev
    block = outer * both
    heads = w_query.shape[1] // width
    columns = w_query.shape[1] + 2 * w_key.shape[1] + LANES

    plans = ([0, 3, 1, 2], [0, 3, 1, 2]) if inner == 4 else (list(range(inner)),) * 2
    gather_plans = ([0, 1, 2, 3], [0, 2, 1, 3]) if inner == 4 else plans
    def exchange(value, steps):
        pairs = [
            (place_from * cores + c, (place_from ^ steps[min(c, 1)]) * cores + c)
            for c in range(cores)
            for place_from in range(devices)
        ]
        return lax.ppermute(value, ("wide", "narrow"), pairs)

    def placed(space, *values):
        return [pltpu.with_memory_space_constraint(value, space) for value in values]

    chunks = w_query.shape[1] // CHUNK
    types = [F32] * inner
    near_far = pl.pallas_call(
        functools.partial(project_kernel, rows_dev, outer, plans),
        out_shape=[jax.ShapeDtypeStruct((both, columns), kind) for kind in types]
        + [jax.ShapeDtypeStruct((block - both, columns), kind) for kind in types],
        in_specs=[whole(pltpu.HBM)] * 6,
        out_specs=[whole()] * (2 * inner),
        scratch_shapes=[
            pltpu.VMEM((chunks, depth, CHUNK), BF16),
            pltpu.VMEM(w_key.shape, BF16),
            pltpu.VMEM(w_value.shape, BF16),
            pltpu.VMEM((2 * rows, depth), BF16),
            pltpu.VMEM((depth,), BF16),
            pltpu.VMEM((2 * rows, depth), BF16),
            pltpu.SemaphoreType.DMA((chunks + 5,)),
        ],
        compiler_params=pltpu.CompilerParams(vmem_limit_bytes=24 * MIB),
        cost_estimate=pl.CostEstimate(
            flops=4 * rows * depth * columns,
            bytes_accessed=2 * depth * columns,
            transcendentals=0,
        ),
        name="project",
    )(*placed(pltpu.HBM, first_input, second_input, norm_gain, w_query, w_key, w_value))

    def spread(values, steps):
        return [
            exchange(value, (steps[0][index + 1], steps[1][index + 1]))
            for index, value in enumerate(values)
        ]

    def narrowed(values):
        return [value.astype(LINK) for value in values]

    far = [value.astype(F32) for value in spread(narrowed(near_far[inner + 1 :]), plans)]
    near = [value.astype(F32) for value in spread(narrowed(near_far[1:inner]), plans)]
    sends = pl.pallas_call(
        functools.partial(combine_kernel, inner - 1),
        out_shape=[jax.ShapeDtypeStruct((both, columns), F32)] * (outer - 1),
        in_specs=[whole()] * inner,
        out_specs=[whole()] * (outer - 1),
        compiler_params=pltpu.CompilerParams(vmem_limit_bytes=16 * MIB),
        name="combine",
    )(near_far[inner], *far)
    received = near + [
        exchange(send, (inner * (index + 1),) * 2).astype(F32)
        for index, send in enumerate(narrowed(sends))
    ]

    cosine, sine = rotary(positions, width)
    slot = lax.broadcasted_iota(jnp.int32, (rows_dev, slots), 1)
    bias = jnp.where(slot < lengths[:, None], 0.0, NEGATIVE)
    attended = pl.pallas_call(
        functools.partial(attend_kernel, len(received), devices * depth),
        out_shape=jax.ShapeDtypeStruct((both, heads * width), BF16),
        in_specs=[whole()] * (len(received) + 6),
        out_specs=whole(),
        scratch_shapes=[
            pltpu.VMEM((heads, both, width), F32),
            pltpu.VMEM((kv_heads, 2 * both, width), BF16),
            pltpu.VMEM((kv_heads, 2 * both, width), BF16),
            pltpu.VMEM((heads, both, width), F32),
            pltpu.VMEM((rows_dev, 2 * heads, slots), F32),
            pltpu.VMEM((rows_dev, 2 * heads, slots), BF16),
        ],
        compiler_params=pltpu.CompilerParams(vmem_limit_bytes=32 * MIB),
        name="attend",
    )(bias, near_far[0], *received, cosine, sine, *placed(pltpu.VMEM, key_cache, value_cache))

    far = [exchange(attended, (inner * step,) * 2) for step in range(1, outer)]
    far = jnp.concatenate(far, axis=0)
    own_blocks = spread([attended] * (inner - 2), gather_plans)
    far_blocks = spread([far] * (inner - 2), gather_plans)
    near = jnp.concatenate([attended, far], axis=0)
    last = exchange(near, (gather_plans[0][-1], gather_plans[1][-1]))
    gathered = jnp.concatenate(
        [near] + [block for blocks in zip(own_blocks, far_blocks) for block in blocks] + [last],
        axis=0,
    )
    part = pl.pallas_call(
        functools.partial(output_kernel, rows_dev, outer, gather_plans),
        out_shape=jax.ShapeDtypeStruct((2 * rows, w_output.shape[1]), F32),
        in_specs=[whole()] * 2,
        out_specs=whole(),
        compiler_params=pltpu.CompilerParams(vmem_limit_bytes=24 * MIB),
        name="output",
    )(gathered, *placed(pltpu.VMEM, w_output))
    part = (part * DROP).astype(LINK)
    other = lax.ppermute(part, "narrow", [(c, cores - 1 - c) for c in range(cores)])
    total = (part.astype(F32) + other.astype(F32)) / DROP
    return (
        (first_input.astype(F32) + total[:rows]).astype(BF16),
        (second_input.astype(F32) + total[rows:]).astype(BF16),
    )


def solution(mesh):
    return jax.shard_map(
        on_device,
        mesh=mesh,
        in_specs=(
            P("groups", "wide"),
            P("groups", "wide"),
            P("wide"),
            P("wide", "narrow"),
            P("wide", "narrow"),
            P("wide", "narrow"),
            P("narrow", "wide"),
            P(("groups", "wide"), "narrow", None, None),
            P(("groups", "wide"), "narrow", None, None),
            P(("groups", "wide")),
            P(("groups", "wide")),
        ),
        out_specs=(P("groups", "wide"), P("groups", "wide")),
        check_vma=False,
    )
```
